512 devices in a mesh: dp: 16 (over y, core), ctx: 32 (over z, x).
Axes of the slice: x: 4, y: 8, z: 8, core: 2. Of those that a mesh axis runs over, the one named last changes fastest.
Arguments:
- query_rows: bfloat16 [65536, 4096], P(('dp', 'ctx')), may hold values from -108 to 108
- rotated_key_rows: bfloat16 [65536, 1024], P(('dp', 'ctx')), may hold values from -4 to 4
- value_head_rows: bfloat16 [65536, 1024], P(('dp', 'ctx')), may hold values from -6 to 6
- doc_lengths: int32 [16, 1, 8], P('dp'), may hold values from 1 to 2048, 4096 in all within a row
- send_slot_index: int32 [16, 32, 192], P('dp', 'ctx'), may hold values from 0 to 128, as said below
- slab_source_index: int32 [16, 32, 128], P('dp', 'ctx'), may hold values from 0 to 191, as said below
- back_pack: int32 [16, 32, 192], P('dp', 'ctx'), may hold values from 0 to 128, as said below
- back_index: int32 [16, 32, 128], P('dp', 'ctx'), may hold values from 0 to 191, as said below
Outputs:
- attention_out: bfloat16 [65536, 4096], P(('dp', 'ctx'))
The draws below stay inside these ranges and needn't reach their ends.
Inputs may be any that keep to these rules, and one draw needn't show every extreme that they name: `send_slot_index`: in each slab every row 0 to 127 appears once; slot block j (slots j * 12 onward) holds the rows sent to slab (j, c), used slots first and 128 in the others; at most 12 rows go from one slab to one slab, and some slab sends exactly 12. `slab_source_index`: names every used received slot of the slab once, as source times 12 plus slot. `back_pack`: sends every placed row back to the slab and slot it came from: entries 128 mark the slots that send_slot_index left empty. `back_index`: names for every row the slot in which it returns.
All inputs are finite; a program needn't handle non-finite values.
Results may differ from the reference program's by a relative error of at most 0.0036.
Values may be sent and summed in bfloat16 or wider, within the bound.
No kernel may reach another device: no remote copies, remote signals or barrier semaphores. Data moves between devices by JAX's collectives and lax.ppermute only.
A program may use at most 128 MiB of HBM per device.

```python
import math
import jax
import jax.numpy as jnp
import numpy as np
from jax import lax

QUERY_HEADS = 32
KEY_VALUE_HEADS = 8
HEAD_SIZE = 128
TOK_DEV = 128
DOCS = 8
PACKS = 1
PACK_ROWS = 4096
TOKEN_TOTAL = 65536
CAP = 12
MOST = 2048
N_DP = 16
N_CTX = 32


def shared_keys(key):
    gaussian_draws = jax.random.normal(key, (TOKEN_TOTAL, KEY_VALUE_HEADS * HEAD_SIZE), jnp.float32)
    return jnp.clip(gaussian_draws, -4.0, 4.0)


def draw_rotated_key_rows(key, part):
    kept_rows = shared_keys(key)
    key = jax.random.fold_in(key, 3)
    return kept_rows.astype(jnp.bfloat16)


def draw_query_rows(key, part):
    key = jax.random.fold_in(key, 5)
    drawn = jnp.clip(jax.random.normal(key, (TOKEN_TOTAL, QUERY_HEADS * HEAD_SIZE), jnp.float32), -4.0, 4.0)
    return drawn.astype(jnp.bfloat16)


def plan_column(key):
    column_keys = jax.random.split(key, 4)
    unit_rows = TOK_DEV // (2 * N_DP)
    pattern = jnp.tile(jnp.array([3, 2, 2, 1], jnp.int32) * unit_rows, N_DP // 4)
    weights = jax.random.permutation(column_keys[0], pattern).astype(jnp.int32)
    shifts = jax.random.permutation(column_keys[1], N_DP).astype(jnp.int32)
    source = jnp.arange(N_DP, dtype=jnp.int32)[:, None]
    target = jnp.arange(N_DP, dtype=jnp.int32)[None, :]
    counts = weights[(shifts[target] - source) % N_DP]
    send_perm = jax.vmap(lambda sub_key: jax.random.permutation(sub_key, TOK_DEV))(jax.random.split(column_keys[2], N_DP)).astype(jnp.int32)
    recv_perm = jax.vmap(lambda sub_key: jax.random.permutation(sub_key, TOK_DEV))(jax.random.split(column_keys[3], N_DP)).astype(jnp.int32)
    send_start = jnp.cumsum(counts, axis=1) - counts
    recv_start = jnp.cumsum(counts, axis=0) - counts
    slot_ids = jnp.arange(CAP, dtype=jnp.int32)[None, None, :]
    source_three = jnp.arange(N_DP, dtype=jnp.int32)[:, None, None]
    target_three = jnp.arange(N_DP, dtype=jnp.int32)[None, :, None]
    filled = slot_ids < counts[:, :, None]
    send_place = jnp.minimum(send_start[:, :, None] + slot_ids, TOK_DEV - 1)
    recv_place = jnp.minimum(recv_start[:, :, None] + slot_ids, TOK_DEV - 1)
    src_row = send_perm[source_three, send_place]
    dst_row = recv_perm[target_three, recv_place]
    empty_row = jnp.int32(TOK_DEV)
    pack_table = jnp.where(filled, src_row, empty_row).reshape(N_DP, N_DP * CAP)
    back_table = jnp.transpose(jnp.where(filled, dst_row, empty_row), (1, 0, 2)).reshape(N_DP, N_DP * CAP)
    dummy_spot = N_DP * TOK_DEV
    forward_code = jnp.broadcast_to(source_three * CAP + slot_ids, filled.shape)
    forward_spot = jnp.where(filled, target_three * TOK_DEV + dst_row, dummy_spot)
    gather_table = jnp.zeros((dummy_spot + 1,), jnp.int32).at[forward_spot.reshape(-1)].set(forward_code.reshape(-1))
    gather_table = gather_table[:dummy_spot].reshape(N_DP, TOK_DEV)
    backward_code = jnp.broadcast_to(target_three * CAP + slot_ids, filled.shape)
    backward_spot = jnp.where(filled, source_three * TOK_DEV + src_row, dummy_spot)
    return_table = jnp.zeros((dummy_spot + 1,), jnp.int32).at[backward_spot.reshape(-1)].set(backward_code.reshape(-1))
    return_table = return_table[:dummy_spot].reshape(N_DP, TOK_DEV)
    return (pack_table, gather_table, back_table, return_table)


def plan_tables(key):
    column_keys = jax.vmap(lambda column: jax.random.fold_in(key, column))(jnp.arange(N_CTX, dtype=jnp.int32))
    tables = jax.vmap(plan_column)(column_keys)
    return tuple((jnp.transpose(table, (1, 0, 2)) for table in tables))


def draw_send_slot_index(key, part):
    tables = plan_tables(key)
    key = jax.random.fold_in(key, 7)
    return tables[0]


def draw_slab_source_index(key, part):
    tables = plan_tables(key)
    key = jax.random.fold_in(key, 11)
    return tables[1]


def draw_back_pack(key, part):
    tables = plan_tables(key)
    key = jax.random.fold_in(key, 13)
    return tables[2]


def draw_back_index(key, part):
    tables = plan_tables(key)
    key = jax.random.fold_in(key, 17)
    return tables[3]


def level_of(rng, shape, cuts, least, top_value):
    level, own = 1.0, jax.random.fold_in(rng, 6)
    for position, parts in cuts:
        draws = jnp.exp(jax.random.uniform(jax.random.fold_in(own, position), (parts,), jnp.float32, least / len(cuts), top_value / len(cuts)))
        level = level * jnp.repeat(draws, shape[position] // parts).reshape([-1 if axis == position else 1 for axis in range(len(shape))])
    return level


def length_profile(count, total, reach, slope):
    loads = [(1 << 20) // math.isqrt(rank ** slope) + 1 for rank in range(2, count + 1)]
    rest, holding = total - reach - (count - 1), [1] * (count - 1)
    while rest > 0:
        free = [i for i in range(count - 1) if holding[i] < reach]
        pool, budget = sum([loads[i] for i in free]), rest
        for i in free:
            addition = min(reach - holding[i], max(1, budget * loads[i] // pool), rest)
            holding[i] = holding[i] + addition
            rest = rest - addition
    return np.array([reach] + holding)


def ragged(rng, number_of, total, bound, lean):
    if number_of == 2:
        one = jax.random.randint(rng, (), max(1, total - bound), min(bound, total - 1) + 1)
        return jnp.stack([one, total - one])
    sizes = jnp.asarray(length_profile(number_of, total, bound, lean), jnp.int32)
    twos = (number_of - 1) // 2
    giver, sink = sizes[1:1 + 2 * twos:2], sizes[2:2 + 2 * twos:2]
    slack = jnp.minimum(giver - 1, bound - sink)
    moved = jax.random.randint(jax.random.fold_in(rng, 1), (twos,), 0, 1 << 20) % (slack + 1)
    sizes = sizes.at[1:1 + 2 * twos:2].set(giver - moved).at[2:2 + 2 * twos:2].set(sink + moved)
    return sizes[jax.random.permutation(jax.random.fold_in(rng, 2), number_of)]


def centred(rng, dims, scale, reach, pieces=(), kind=jnp.bfloat16):
    values = scale * jax.random.normal(rng, dims, jnp.float32)
    if pieces:
        values = values * level_of(rng, dims, pieces, -0.22, 0.18)
    return jnp.clip(values, -reach, reach).astype(kind)


def setup_inputs(seed: int = 0) -> dict:
    keys = jax.random.split(jax.random.key(seed), 9)
    query_rows = draw_query_rows(jax.random.fold_in(keys[8], 71), 0)
    rotated_key_rows = draw_rotated_key_rows(jax.random.fold_in(keys[8], 71), 0)
    value_head_rows = centred(keys[2], (TOKEN_TOTAL, KEY_VALUE_HEADS * HEAD_SIZE), 1.0, 6.0, ((0, 512),))
    doc_lengths = jax.vmap(lambda own: ragged(own, DOCS, PACK_ROWS, MOST, 2))(jax.random.split(keys[3], N_DP * PACKS)).reshape((N_DP, PACKS, DOCS)).astype(jnp.int32)
    send_slot_index = draw_send_slot_index(jax.random.fold_in(keys[8], 71), 0)
    slab_source_index = draw_slab_source_index(jax.random.fold_in(keys[8], 71), 0)
    back_pack = draw_back_pack(jax.random.fold_in(keys[8], 71), 0)
    back_index = draw_back_index(jax.random.fold_in(keys[8], 71), 0)
    return {"query_rows": query_rows, "rotated_key_rows": rotated_key_rows, "value_head_rows": value_head_rows, "doc_lengths": doc_lengths, "send_slot_index": send_slot_index, "slab_source_index": slab_source_index, "back_pack": back_pack, "back_index": back_index}


def document_ids(lengths, pack_rows):
    bounds = jnp.cumsum(lengths.astype(jnp.int32))
    places = jnp.arange(pack_rows, dtype=jnp.int32)
    return lax.optimization_barrier(jnp.sum((places[:, None] >= bounds[None, :]).astype(jnp.int32), axis=1)).astype(jnp.int32)

def rebalance_rows(slabs, send_table, lookup_table):
    width = slabs.shape[-1]
    padded = jnp.concatenate([slabs, jnp.zeros_like(slabs[:, :, :1])], axis=2)
    pick = jax.vmap(jax.vmap(lambda rows_per_slab, row_table: rows_per_slab[row_table]))
    sent = pick(padded, send_table.astype(jnp.int32))
    sent = sent.reshape(N_DP, N_CTX, N_DP, CAP, width)
    arrived = jnp.transpose(sent, (2, 1, 0, 3, 4)).reshape(N_DP, N_CTX, N_DP * CAP, width)
    return pick(arrived, lookup_table.astype(jnp.int32))

def attend_pack(operands):
    head_q, key_per_head, value_per_head, lengths = operands
    pack_rows = head_q.shape[0]
    doc_ids = document_ids(lengths, pack_rows)
    head_q = head_q.astype(jnp.float32)
    key_per_head = jnp.repeat(key_per_head, QUERY_HEADS // KEY_VALUE_HEADS, axis=1).astype(jnp.float32)
    value_per_head = jnp.repeat(value_per_head, QUERY_HEADS // KEY_VALUE_HEADS, axis=1).astype(jnp.float32)
    score_scale = 1.0 / math.sqrt(HEAD_SIZE)
    tile_rows = min(512, pack_rows)
    outputs = []
    for block_index in range(pack_rows // tile_rows):
        start_row = block_index * tile_rows
        end_row = start_row + tile_rows
        scores = jnp.einsum('qhe,khe->hqk', head_q[start_row:end_row], key_per_head[:end_row]) * score_scale
        query_at = start_row + jnp.arange(tile_rows, dtype=jnp.int32)
        key_at = jnp.arange(end_row, dtype=jnp.int32)
        allowed = (doc_ids[start_row:end_row][:, None] == doc_ids[:end_row][None, :]) & (key_at[None, :] <= query_at[:, None])
        scores = jnp.where(allowed[None], scores, -jnp.inf)
        row_max = lax.optimization_barrier(jnp.max(scores, axis=2, keepdims=True))
        weights = jnp.exp(scores - row_max)
        totals = lax.optimization_barrier(jnp.sum(weights, axis=2))
        probabilities = lax.optimization_barrier(weights.astype(jnp.bfloat16)).astype(jnp.float32)
        weighted = jnp.einsum('hqk,khe->qhe', probabilities, value_per_head[:end_row])
        outputs.append((weighted / jnp.transpose(totals)[:, :, None]).astype(jnp.bfloat16))
    return jnp.concatenate(outputs, axis=0)

def reference(query_rows, rotated_key_rows, value_head_rows, doc_lengths, send_slot_index, slab_source_index, back_pack, back_index):

    def split_into_slabs(source):
        return source.reshape(N_DP, N_CTX, TOK_DEV, source.shape[1])
    pack_count = N_DP * PACKS
    placed_q = rebalance_rows(split_into_slabs(query_rows), send_slot_index, slab_source_index).reshape(pack_count, PACK_ROWS, QUERY_HEADS, HEAD_SIZE)
    arranged_keys = rebalance_rows(split_into_slabs(rotated_key_rows), send_slot_index, slab_source_index).reshape(pack_count, PACK_ROWS, KEY_VALUE_HEADS, HEAD_SIZE)
    arranged_values = rebalance_rows(split_into_slabs(value_head_rows), send_slot_index, slab_source_index).reshape(pack_count, PACK_ROWS, KEY_VALUE_HEADS, HEAD_SIZE)
    attended = lax.map(attend_pack, (placed_q, arranged_keys, arranged_values, doc_lengths.reshape(pack_count, DOCS)))
    returned = rebalance_rows(attended.reshape(N_DP, N_CTX, TOK_DEV, QUERY_HEADS * HEAD_SIZE), back_pack, back_index)
    return returned.reshape(TOKEN_TOTAL, QUERY_HEADS * HEAD_SIZE)
```

```python
import math

import jax
import jax.numpy as jnp
from jax import lax
from jax.experimental import pallas as pl
from jax.experimental.pallas import tpu as pltpu
from jax.sharding import Mesh, PartitionSpec as P

QUERY_HEADS = 32
KEY_VALUE_HEADS = 8
HEAD_SIZE = 128
GROUP_HEADS = QUERY_HEADS // KEY_VALUE_HEADS
CAP = 12
N_DP = 16
N_Z = 8
N_X = 4
SLAB = 128
DOCS = 8
MOST = 2048
Q_ROWS = GROUP_HEADS * CAP
KV_ROWS = 2 * CAP
PAIR = 2 * SLAB
MAX_PAIRS = MOST // PAIR + 1
EXP2_SCALE = math.log2(math.e) / math.sqrt(HEAD_SIZE)
MASKED = -1e30
VMEM_BYTES = 40 * 1024 * 1024
EXCHANGE = ("y", "core", "z")


def slot_rows(code, heads):
    peer = (code * 171) >> 11
    base = peer * (heads * CAP) + (code - peer * CAP)
    return jnp.concatenate([base + h * CAP for h in range(heads)], axis=1)


def one_hot(rows, targets):
    at = lax.broadcasted_iota(jnp.int32, (rows, targets.shape[1]), 0)
    return jnp.where(at == targets, 1.0, 0.0).astype(jnp.bfloat16)


def contract(a, b, dim_a, dim_b):
    return lax.dot_general(
        a, b, (((dim_a,), (dim_b,)), ((), ())), preferred_element_type=jnp.float32
    )


def pack_kv_kernel(code_ref, key_ref, value_ref, out_ref):
    select = one_hot(N_DP * KV_ROWS, slot_rows(code_ref[...], 2))
    rows = jnp.concatenate([key_ref[...], value_ref[...]], axis=0)
    sent = contract(select, rows, 1, 0).astype(jnp.bfloat16)
    for z in range(N_Z):
        piece = sent[:, z * HEAD_SIZE : (z + 1) * HEAD_SIZE]
        out_ref[:, z] = piece.reshape(N_DP, KV_ROWS, HEAD_SIZE)


def pack_q_kernel(code_ref, query_ref, out_ref):
    select = one_hot(N_DP * Q_ROWS, slot_rows(code_ref[...], GROUP_HEADS))
    for z in range(N_Z):
        first = z * GROUP_HEADS
        rows = jnp.concatenate(
            [
                query_ref[:, (first + h) * HEAD_SIZE : (first + h + 1) * HEAD_SIZE]
                for h in range(GROUP_HEADS)
            ],
            axis=0,
        )
        sent = contract(select, rows, 1, 0).astype(jnp.bfloat16)
        out_ref[:, z] = sent.reshape(N_DP, Q_ROWS, HEAD_SIZE)


def place_kv_kernel(code_ref, slots_ref, out_ref):
    for z in range(N_Z):
        select = one_hot(N_DP * KV_ROWS, slot_rows(code_ref[z : z + 1, :], 2))
        slots = slots_ref[:, z].reshape(N_DP * KV_ROWS, HEAD_SIZE)
        keys = contract(select[:, :SLAB], slots, 0, 0)
        values_t = contract(slots, select[:, SLAB:], 0, 0)
        out_ref[z, :SLAB] = keys.astype(jnp.bfloat16)
        out_ref[z, SLAB:] = values_t.astype(jnp.bfloat16)


def attend_kernel(lengths_ref, lane_ref, code_ref, slots_ref, kv_ref, out_ref, scores_ref, acc_ref):
    lane = lane_ref[0]
    bounds = []
    total = jnp.int32(0)
    for i in range(DOCS):
        total = total + lengths_ref[i]
        bounds.append(total)
    columns = GROUP_HEADS * SLAB
    in_slab = lax.broadcasted_iota(jnp.int32, (1, columns), 1) & (SLAB - 1)

    def slab(z, carry):
        first = (z * N_X + lane) * SLAB
        query_at = first + in_slab
        start = jnp.zeros((1, columns), jnp.int32)
        first_start = jnp.int32(0)
        for bound in bounds:
            start = jnp.where(query_at >= bound, bound, start)
            first_start = jnp.where(first >= bound, bound, first_start)
        pair_low = first_start // PAIR
        pairs = first // PAIR - pair_low + 1

        select = one_hot(N_DP * Q_ROWS, slot_rows(code_ref[pl.ds(z, 1), :], GROUP_HEADS))
        slots = slots_ref[:, z].reshape(N_DP * Q_ROWS, HEAD_SIZE)
        query_t = contract(slots, select, 0, 0).astype(jnp.bfloat16)

        def score(i, largest):
            pair = pair_low + i
            zk, xk = pair // 2, 2 * (pair % 2)
            keys = jnp.concatenate([kv_ref[xk, zk, :SLAB], kv_ref[xk + 1, zk, :SLAB]], axis=0)
            s = contract(keys, query_t, 1, 0)
            key_at = pair * PAIR + lax.broadcasted_iota(jnp.int32, (PAIR, columns), 0)
            s = jnp.where((key_at >= start) & (key_at <= query_at), s, MASKED)
            scores_ref[i] = s
            return jnp.maximum(largest, jnp.max(s.reshape(PAIR // 8, 8, columns), axis=0))

        largest = lax.fori_loop(0, pairs, score, jnp.full((8, columns), MASKED, jnp.float32))
        shift = jnp.max(largest, axis=0, keepdims=True) * EXP2_SCALE
        acc_ref[...] = jnp.zeros_like(acc_ref)

        def weigh(i, totals):
            pair = pair_low + i
            zk, xk = pair // 2, 2 * (pair % 2)
            weights = jnp.exp2(scores_ref[i] * EXP2_SCALE - shift)
            values_t = jnp.concatenate(
                [kv_ref[xk, zk, SLAB:], kv_ref[xk + 1, zk, SLAB:]], axis=1
            )
            acc_ref[...] += contract(values_t, weights.astype(jnp.bfloat16), 1, 0)
            return totals + jnp.sum(weights.reshape(PAIR // 8, 8, columns), axis=0)

        totals = lax.fori_loop(0, pairs, weigh, jnp.zeros((8, columns), jnp.float32))
        totals = jnp.sum(totals, axis=0, keepdims=True)
        attended_t = (acc_ref[...] / totals).astype(jnp.bfloat16)
        back = contract(select, attended_t, 1, 1).astype(jnp.bfloat16)
        out_ref[:, z] = back.reshape(N_DP, Q_ROWS, HEAD_SIZE)
        return carry

    lax.fori_loop(0, N_Z, slab, 0)


def unpack_kernel(code_ref, slots_ref, out_ref):
    select = one_hot(N_DP * Q_ROWS, slot_rows(code_ref[...], GROUP_HEADS))
    for z in range(N_Z):
        slots = slots_ref[:, z].reshape(N_DP * Q_ROWS, HEAD_SIZE)
        rows = contract(select, slots, 0, 0).astype(jnp.bfloat16)
        for h in range(GROUP_HEADS):
            at = (z * GROUP_HEADS + h) * HEAD_SIZE
            out_ref[:, at : at + HEAD_SIZE] = rows[h * SLAB : (h + 1) * SLAB]


def call(kernel, name, out_shape, specs, flops, moved, exps=0, scratch=()):
    return pl.pallas_call(
        kernel,
        name=name,
        out_shape=jax.ShapeDtypeStruct(out_shape, jnp.bfloat16),
        in_specs=[pl.BlockSpec(memory_space=s) for s in specs],
        out_specs=pl.BlockSpec(memory_space=pltpu.VMEM),
        scratch_shapes=scratch,
        compiler_params=pltpu.CompilerParams(vmem_limit_bytes=VMEM_BYTES),
        cost_estimate=pl.CostEstimate(flops=flops, bytes_accessed=moved, transcendentals=exps),
    )


def exchange(blocks):
    flat = blocks.reshape((N_DP * N_Z,) + blocks.shape[2:])
    flat = lax.all_to_all(flat, EXCHANGE, split_axis=0, concat_axis=0, tiled=True)
    return flat.reshape(blocks.shape)


def local(query, key, value, doc_lengths, send_slots, slab_source, back_pack, back_index):
    V, S = pltpu.VMEM, pltpu.SMEM
    columns = GROUP_HEADS * SLAB
    own_code = back_index.reshape(1, SLAB)
    q_blocks = (N_DP, N_Z, Q_ROWS, HEAD_SIZE)
    kv_blocks = (N_DP, N_Z, KV_ROWS, HEAD_SIZE)
    kv_sent = call(pack_kv_kernel, "pack_kv", kv_blocks, [V, V, V], 2 * 10**8, 2 * 10**6)(
        own_code, key, value
    )
    placed_code = lax.all_gather(slab_source.reshape(1, SLAB), "z", axis=0, tiled=True)
    kv_slots = exchange(kv_sent)
    q_sent = call(pack_q_kernel, "pack_q", q_blocks, [V, V], 8 * 10**8, 3 * 10**6)(
        own_code, query
    )
    q_sent, kv_slots = lax.optimization_barrier((q_sent, kv_slots))
    q_slots = exchange(q_sent)
    kv_placed = call(
        place_kv_kernel, "place_kv", (N_Z, 2 * SLAB, HEAD_SIZE), [V, V], 2 * 10**8, 2 * 10**6
    )(placed_code, kv_slots)
    kv_all = lax.all_gather(kv_placed, "x", axis=0, tiled=False)
    lane = lax.axis_index("x").astype(jnp.int32).reshape(1)
    out_sent = call(
        attend_kernel,
        "attend",
        q_blocks,
        [S, S, V, V, V],
        4 * 10**9,
        5 * 10**6,
        3 * 10**6,
        [
            pltpu.VMEM((MAX_PAIRS, PAIR, columns), jnp.float32),
            pltpu.VMEM((HEAD_SIZE, columns), jnp.float32),
        ],
    )(doc_lengths.reshape(DOCS), lane, placed_code, q_slots, kv_all)
    out_slots = exchange(out_sent)
    return call(
        unpack_kernel, "unpack", (SLAB, QUERY_HEADS * HEAD_SIZE), [V, V], 8 * 10**8, 3 * 10**6
    )(own_code, out_slots)


def solution(mesh):
    wide = Mesh(mesh.devices.reshape(N_DP // 2, 2, N_Z, N_X), ("y", "core", "z", "x"))
    rows = P(("y", "core", "z", "x"), None)
    table = P(("y", "core"), ("z", "x"), None)
    return jax.shard_map(
        local,
        mesh=wide,
        in_specs=(rows, rows, rows, P(("y", "core"), None, None), table, table, table, table),
        out_specs=rows,
        check_vma=False,
    )
```

```python
import math

import jax
import jax.numpy as jnp
from jax import lax
from jax.experimental import pallas as pl
from jax.experimental.pallas import tpu as pltpu
from jax.sharding import Mesh, PartitionSpec as P

QUERY_HEADS = 32
KEY_VALUE_HEADS = 8
HEAD_SIZE = 128
GROUP_HEADS = QUERY_HEADS // KEY_VALUE_HEADS
CAP = 12
N_DP = 16
N_Z = 8
N_X = 4
SLAB = 128
DOCS = 8
MOST = 2048
Q_ROWS = GROUP_HEADS * CAP
TABLE_AT = 2 * CAP
KV_ROWS = 32
PAIR = 2 * SLAB
MAX_PAIRS = MOST // PAIR + 1
STEPS = (4, 2, 1)
EXP2_SCALE = math.log2(math.e) / math.sqrt(HEAD_SIZE)
MASKED = -1e30
VMEM_BYTES = 24 * 1024 * 1024
EXCHANGE = ("y", "core", "z")


def slot_rows(code, heads, block_rows):
    peer = (code * 171) >> 11
    base = peer * block_rows + (code - peer * CAP)
    return jnp.concatenate([base + h * CAP for h in range(heads)], axis=1)


def one_hot(rows, targets):
    at = lax.broadcasted_iota(jnp.int32, (rows, targets.shape[1]), 0)
    return jnp.where(at == targets, 1.0, 0.0).astype(jnp.bfloat16)


def contract(a, b, dim_a, dim_b):
    return lax.dot_general(
        a, b, (((dim_a,), (dim_b,)), ((), ())), preferred_element_type=jnp.float32
    )


def pack_kv_kernel(
    code_ref, table_ref, key_ref, value_ref, out_ref, code, table, rows, sems
):
    copies = [
        pltpu.make_async_copy(code_ref, code, sems.at[0]),
        pltpu.make_async_copy(table_ref, table, sems.at[1]),
        pltpu.make_async_copy(key_ref, rows.at[:SLAB], sems.at[2]),
        pltpu.make_async_copy(value_ref, rows.at[SLAB:], sems.at[3]),
    ]
    for copy in copies:
        copy.start()
    for copy in copies:
        copy.wait()
    select = one_hot(N_DP * TABLE_AT, slot_rows(code[0], 2, TABLE_AT))
    sent = contract(select, rows[...], 1, 0).astype(jnp.bfloat16)
    codes = jnp.broadcast_to(
        table[0].astype(jnp.float32).astype(jnp.bfloat16)[None],
        (N_DP, KV_ROWS - TABLE_AT, SLAB),
    )
    for z in range(N_Z):
        piece = sent[:, z * HEAD_SIZE : (z + 1) * HEAD_SIZE]
        piece = piece.reshape(N_DP, TABLE_AT, HEAD_SIZE)
        out_ref[:, z] = jnp.concatenate([piece, codes], axis=1)


def pack_q_kernel(code_ref, query_ref, out_ref):
    select = one_hot(N_DP * Q_ROWS, slot_rows(code_ref[...], GROUP_HEADS, Q_ROWS))
    for z in range(N_Z):
        first = z * GROUP_HEADS
        rows = jnp.concatenate(
            [
                query_ref[:, (first + h) * HEAD_SIZE : (first + h + 1) * HEAD_SIZE]
                for h in range(GROUP_HEADS)
            ],
            axis=0,
        )
        sent = contract(select, rows, 1, 0).astype(jnp.bfloat16)
        out_ref[:, z] = sent.reshape(N_DP, Q_ROWS, HEAD_SIZE)


def place_kv_kernel(group_ref, slots_ref, out_ref, code_ref):
    group = group_ref[0]
    for z in range(N_Z):
        code = slots_ref[group, z, TABLE_AT:, :].astype(jnp.float32).astype(jnp.int32)[:1]
        code_ref[z : z + 1, :] = code
        select = one_hot(N_DP * KV_ROWS, slot_rows(code, 2, KV_ROWS))
        slots = slots_ref[:, z].reshape(N_DP * KV_ROWS, HEAD_SIZE)
        keys = contract(select[:, :SLAB], slots, 0, 0)
        values_t = contract(slots, select[:, SLAB:], 0, 0)
        out_ref[z, :SLAB] = keys.astype(jnp.bfloat16)
        out_ref[z, SLAB:] = values_t.astype(jnp.bfloat16)


def order_kv_kernel(gathered_ref, out_ref):
    for block in range(N_Z * N_X):
        z, x = block // N_X, block % N_X
        half = slice((block % 2) * SLAB, (block % 2 + 1) * SLAB)
        out_ref[block // 2, 0, half] = gathered_ref[x, z, :SLAB]
        out_ref[block // 2, 1, half] = gathered_ref[x, z, SLAB:]


def in_steps(count, sizes, body, carry):
    done = jnp.int32(0)
    for size in sizes:
        steps = (count - done) // size if size > 1 else count - done

        def step(i, carry, done=done, size=size):
            return body(done + i * size, size, carry)

        carry = lax.fori_loop(0, steps, step, carry)
        done = done + steps * size
    return carry


def attend_kernel(
    lengths_ref, lane_ref, code_ref, slots_ref, kv_ref, out_ref, scores_ref, acc_ref
):
    lane = lane_ref[0]
    bounds = []
    total = jnp.int32(0)
    for i in range(DOCS):
        total = total + lengths_ref[i]
        bounds.append(total)
    columns = GROUP_HEADS * SLAB
    in_slab = lax.broadcasted_iota(jnp.int32, (1, SLAB), 1)
    in_pair = lax.broadcasted_iota(jnp.int32, (PAIR, SLAB), 0)

    def slab(z, carry):
        first = (z * N_X + lane) * SLAB
        query_at = first + in_slab
        start = jnp.zeros((1, SLAB), jnp.int32)
        first_start = jnp.int32(0)
        for bound in bounds:
            start = jnp.where(query_at >= bound, bound, start)
            first_start = jnp.where(first >= bound, bound, first_start)
        pair_low = first_start // PAIR
        pairs = first // PAIR - pair_low + 1

        select = one_hot(
            N_DP * Q_ROWS, slot_rows(code_ref[pl.ds(z, 1), :], GROUP_HEADS, Q_ROWS)
        )
        slots = slots_ref[:, z].reshape(N_DP * Q_ROWS, HEAD_SIZE)
        query_t = contract(slots, select, 0, 0).astype(jnp.bfloat16)

        def score(i, size, largest):
            for r in range(size):
                at = (pair_low + i + r) * PAIR
                s = contract(kv_ref[pair_low + i + r, 0], query_t, 1, 0)
                allowed = (in_pair >= start - at) & (in_pair <= query_at - at)
                tops = []
                for h in range(GROUP_HEADS):
                    lanes = slice(h * SLAB, (h + 1) * SLAB)
                    masked = jnp.where(allowed, s[:, lanes], MASKED)
                    scores_ref[i + r, :, lanes] = masked
                    tops.append(jnp.max(masked.reshape(PAIR // 8, 8, SLAB), axis=0))
                largest = jnp.maximum(largest, jnp.concatenate(tops, axis=1))
            return largest

        largest = jnp.full((8, columns), MASKED, jnp.float32)
        largest = in_steps(pairs, STEPS, score, largest)
        shift = jnp.max(largest, axis=0, keepdims=True) * EXP2_SCALE
        acc_ref[...] = jnp.zeros_like(acc_ref)

        def weigh(i, size, totals):
            added = None
            for r in range(size):
                weights = jnp.exp2(scores_ref[i + r] * EXP2_SCALE - shift)
                values_t = jnp.concatenate(
                    [
                        kv_ref[pair_low + i + r, 1, :SLAB],
                        kv_ref[pair_low + i + r, 1, SLAB:],
                    ],
                    axis=1,
                )
                part = contract(values_t, weights.astype(jnp.bfloat16), 1, 0)
                added = part if added is None else added + part
                totals = totals + jnp.sum(weights.reshape(PAIR // 8, 8, columns), axis=0)
            acc_ref[...] += added
            return totals

        totals = in_steps(pairs, STEPS, weigh, jnp.zeros((8, columns), jnp.float32))
        totals = jnp.sum(totals, axis=0, keepdims=True)
        attended_t = (acc_ref[...] / totals).astype(jnp.bfloat16)
        back = contract(select, attended_t, 1, 1).astype(jnp.bfloat16)
        out_ref[:, z] = back.reshape(N_DP, Q_ROWS, HEAD_SIZE)
        return carry

    lax.fori_loop(0, N_Z, slab, 0)


def unpack_kernel(targets_ref, slots_ref, out_ref):
    select = one_hot(GROUP_HEADS * SLAB, targets_ref[...])
    for z in range(N_Z):
        slots = slots_ref[:, z].reshape(N_DP * Q_ROWS, HEAD_SIZE)
        rows = contract(select, slots, 1, 0).astype(jnp.bfloat16)
        for h in range(GROUP_HEADS):
            at = (z * GROUP_HEADS + h) * HEAD_SIZE
            out_ref[:, at : at + HEAD_SIZE] = rows[h * SLAB : (h + 1) * SLAB]


def call(kernel, name, outs, specs, flops, moved, exps=0, scratch=(), vmem=VMEM_BYTES):
    return pl.pallas_call(
        kernel,
        name=name,
        out_shape=[jax.ShapeDtypeStruct(shape, dtype) for shape, dtype in outs],
        in_specs=[pl.BlockSpec(memory_space=s) for s in specs],
        out_specs=[pl.BlockSpec(memory_space=pltpu.VMEM)] * len(outs),
        scratch_shapes=scratch,
        compiler_params=pltpu.CompilerParams(vmem_limit_bytes=vmem),
        cost_estimate=pl.CostEstimate(flops=flops, bytes_accessed=moved, transcendentals=exps),
    )


def exchange(blocks):
    flat = blocks.reshape((N_DP * N_Z,) + blocks.shape[2:])
    flat = lax.all_to_all(flat, EXCHANGE, split_axis=0, concat_axis=0, tiled=True)
    return flat.reshape(blocks.shape)


def local(query, key, value, doc_lengths, send_slots, slab_source, back_pack, back_index):
    V, S, H = pltpu.VMEM, pltpu.SMEM, pl.ANY
    half, whole = jnp.bfloat16, jnp.int32
    columns = GROUP_HEADS * SLAB
    q_blocks = (N_DP, N_Z, Q_ROWS, HEAD_SIZE)
    kv_blocks = (N_DP, N_Z, KV_ROWS, HEAD_SIZE)
    (kv_sent,) = call(
        pack_kv_kernel,
        "pack_kv",
        [(kv_blocks, half)],
        [H, H, H, H],
        2 * 10**8,
        2 * 10**6,
        0,
        [
            V((1, 1, SLAB), whole),
            V((1, 1, SLAB), whole),
            V((2 * SLAB, KEY_VALUE_HEADS * HEAD_SIZE), half),
            pltpu.SemaphoreType.DMA((4,)),
        ],
        60 * 1024 * 1024,
    )(back_index, slab_source, key, value)
    kv_slots = exchange(kv_sent)
    own_code = back_index.reshape(1, SLAB)
    (q_sent,) = call(pack_q_kernel, "pack_q", [(q_blocks, half)], [V, V], 8 * 10**8, 3 * 10**6)(
        own_code, query
    )
    q_sent, kv_slots = lax.optimization_barrier((q_sent, kv_slots))
    q_slots = exchange(q_sent)
    group = lax.axis_index(("y", "core")).astype(whole).reshape(1)
    kv_placed, code = call(
        place_kv_kernel,
        "place_kv",
        [((N_Z, 2 * SLAB, HEAD_SIZE), half), ((N_Z, SLAB), whole)],
        [S, V],
        2 * 10**8,
        2 * 10**6,
    )(group, kv_slots)
    kv_all = lax.all_gather(kv_placed, "x", axis=0, tiled=False)
    (kv_pairs,) = call(
        order_kv_kernel,
        "order_kv",
        [((N_Z * N_X // 2, 2, PAIR, HEAD_SIZE), half)],
        [V],
        10**6,
        4 * 10**6,
    )(kv_all)
    lane = lax.axis_index("x").astype(whole).reshape(1)
    (out_sent,) = call(
        attend_kernel,
        "attend",
        [(q_blocks, half)],
        [S, S, V, V, V],
        4 * 10**9,
        5 * 10**6,
        3 * 10**6,
        [V((MAX_PAIRS, PAIR, columns), jnp.float32), V((HEAD_SIZE, columns), jnp.float32)],
    )(doc_lengths.reshape(DOCS), lane, code, q_slots, kv_pairs)
    out_slots = exchange(out_sent)
    sent = send_slots.reshape(N_DP, 1, CAP)
    head = jnp.arange(GROUP_HEADS, dtype=whole).reshape(1, GROUP_HEADS, 1)
    targets = jnp.where(sent < SLAB, sent + head * SLAB, -1).reshape(1, N_DP * Q_ROWS)
    (out,) = call(
        unpack_kernel,
        "unpack",
        [((SLAB, QUERY_HEADS * HEAD_SIZE), half)],
        [V, V],
        8 * 10**8,
        3 * 10**6,
    )(targets, out_slots)
    return out


def solution(mesh):
    wide = Mesh(mesh.devices.reshape(N_DP // 2, 2, N_Z, N_X), ("y", "core", "z", "x"))
    rows = P(("y", "core", "z", "x"), None)
    table = P(("y", "core"), ("z", "x"), None)
    return jax.shard_map(
        local,
        mesh=wide,
        in_specs=(rows, rows, rows, P(("y", "core"), None, None), table, table, table, table),
        out_specs=rows,
        check_vma=False,
    )
```

```python
import math

import jax
import jax.numpy as jnp
from jax import lax
from jax.experimental import pallas as pl
from jax.experimental.pallas import tpu as pltpu
from jax.sharding import Mesh, PartitionSpec as P

QUERY_HEADS = 32
KEY_VALUE_HEADS = 8
HEAD_SIZE = 128
GROUP_HEADS = QUERY_HEADS // KEY_VALUE_HEADS
CAP = 12
N_DP = 16
N_Z = 8
N_X = 4
SLAB = 128
DOCS = 8
MOST = 2048
Q_ROWS = GROUP_HEADS * CAP
TABLE_AT = 2 * CAP
KV_ROWS = 32
PAIR = 2 * SLAB
MAX_PAIRS = MOST // PAIR + 1
STEPS = (4, 2, 1)
EXP2_SCALE = math.log2(math.e) / math.sqrt(HEAD_SIZE)
MASKED = -1e30
VMEM_BYTES = 24 * 1024 * 1024
EXCHANGE = ("y", "core", "z")


def slot_rows(code, heads, block_rows):
    peer = (code * 171) >> 11
    base = peer * block_rows + (code - peer * CAP)
    return jnp.concatenate([base + h * CAP for h in range(heads)], axis=1)


def one_hot(rows, targets):
    at = lax.broadcasted_iota(jnp.int32, (rows, targets.shape[1]), 0)
    return jnp.where(at == targets, 1.0, 0.0).astype(jnp.bfloat16)


def contract(a, b, dim_a, dim_b):
    return lax.dot_general(
        a, b, (((dim_a,), (dim_b,)), ((), ())), preferred_element_type=jnp.float32
    )


def pack_kv_kernel(
    code_ref, table_ref, key_ref, value_ref, out_ref, code, table, rows, sems
):
    copies = [
        pltpu.make_async_copy(code_ref, code, sems.at[0]),
        pltpu.make_async_copy(table_ref, table, sems.at[1]),
        pltpu.make_async_copy(key_ref, rows.at[:SLAB], sems.at[2]),
        pltpu.make_async_copy(value_ref, rows.at[SLAB:], sems.at[3]),
    ]
    for copy in copies:
        copy.start()
    for copy in copies:
        copy.wait()
    select = one_hot(N_DP * TABLE_AT, slot_rows(code[0], 2, TABLE_AT))
    sent = contract(select, rows[...], 1, 0).astype(jnp.bfloat16)
    codes = jnp.broadcast_to(
        table[0].astype(jnp.float32).astype(jnp.bfloat16)[None],
        (N_DP, KV_ROWS - TABLE_AT, SLAB),
    )
    for z in range(N_Z):
        piece = sent[:, z * HEAD_SIZE : (z + 1) * HEAD_SIZE]
        piece = piece.reshape(N_DP, TABLE_AT, HEAD_SIZE)
        out_ref[:, z] = jnp.concatenate([piece, codes], axis=1)


def pack_q_kernel(code_ref, query_ref, out_ref):
    select = one_hot(N_DP * Q_ROWS, slot_rows(code_ref[...], GROUP_HEADS, Q_ROWS))
    for z in range(N_Z):
        first = z * GROUP_HEADS
        rows = jnp.concatenate(
            [
                query_ref[:, (first + h) * HEAD_SIZE : (first + h + 1) * HEAD_SIZE]
                for h in range(GROUP_HEADS)
            ],
            axis=0,
        )
        sent = contract(select, rows, 1, 0).astype(jnp.bfloat16)
        out_ref[:, z] = sent.reshape(N_DP, Q_ROWS, HEAD_SIZE)


def place_kv_kernel(group_ref, slots_ref, out_ref, code_ref):
    group = group_ref[0]
    for z in range(N_Z):
        code = slots_ref[group, z, TABLE_AT:, :].astype(jnp.float32).astype(jnp.int32)[:1]
        code_ref[z : z + 1, :] = code
        select = one_hot(N_DP * KV_ROWS, slot_rows(code, 2, KV_ROWS))
        slots = slots_ref[:, z].reshape(N_DP * KV_ROWS, HEAD_SIZE)
        keys = contract(select[:, :SLAB], slots, 0, 0)
        values_t = contract(slots, select[:, SLAB:], 0, 0)
        out_ref[z, :SLAB] = keys.astype(jnp.bfloat16)
        out_ref[z, SLAB:] = values_t.astype(jnp.bfloat16)


def order_kv_kernel(lane_ref, *refs):
    out_ref = refs[N_X]
    for back, piece_ref in enumerate(refs[:N_X]):
        x = (lane_ref[0] - back) & (N_X - 1)
        for z in range(N_Z):
            out_ref[z * N_X + x] = piece_ref[z]


def in_steps(count, sizes, body, carry):
    done = jnp.int32(0)
    for size in sizes:
        steps = (count - done) // size if size > 1 else count - done

        def step(i, carry, done=done, size=size):
            return body(done + i * size, size, carry)

        carry = lax.fori_loop(0, steps, step, carry)
        done = done + steps * size
    return carry


def attend_kernel(
    lengths_ref, lane_ref, code_ref, slots_ref, kv_ref, out_ref, scores_ref, acc_ref
):
    lane = lane_ref[0]
    bounds = []
    total = jnp.int32(0)
    for i in range(DOCS):
        total = total + lengths_ref[i]
        bounds.append(total)
    columns = GROUP_HEADS * SLAB
    in_slab = lax.broadcasted_iota(jnp.int32, (1, SLAB), 1)
    in_pair = lax.broadcasted_iota(jnp.int32, (PAIR, SLAB), 0)

    def slab(z, carry):
        first = (z * N_X + lane) * SLAB
        query_at = first + in_slab
        start = jnp.zeros((1, SLAB), jnp.int32)
        first_start = jnp.int32(0)
        for bound in bounds:
            start = jnp.where(query_at >= bound, bound, start)
            first_start = jnp.where(first >= bound, bound, first_start)
        pair_low = first_start // PAIR
        pairs = first // PAIR - pair_low + 1

        select = one_hot(
            N_DP * Q_ROWS, slot_rows(code_ref[pl.ds(z, 1), :], GROUP_HEADS, Q_ROWS)
        )
        slots = slots_ref[:, z].reshape(N_DP * Q_ROWS, HEAD_SIZE)
        query_t = contract(slots, select, 0, 0).astype(jnp.bfloat16)

        def score(i, size, largest):
            for r in range(size):
                at = (pair_low + i + r) * PAIR
                block = 2 * (pair_low + i + r)
                keys = jnp.concatenate([kv_ref[block, :SLAB], kv_ref[block + 1, :SLAB]], axis=0)
                s = contract(keys, query_t, 1, 0)
                allowed = (in_pair >= start - at) & (in_pair <= query_at - at)
                tops = []
                for h in range(GROUP_HEADS):
                    lanes = slice(h * SLAB, (h + 1) * SLAB)
                    masked = jnp.where(allowed, s[:, lanes], MASKED)
                    scores_ref[i + r, :, lanes] = masked
                    tops.append(jnp.max(masked.reshape(PAIR // 8, 8, SLAB), axis=0))
                largest = jnp.maximum(largest, jnp.concatenate(tops, axis=1))
            return largest

        largest = jnp.full((8, columns), MASKED, jnp.float32)
        largest = in_steps(pairs, STEPS, score, largest)
        shift = jnp.max(largest, axis=0, keepdims=True) * EXP2_SCALE
        acc_ref[...] = jnp.zeros_like(acc_ref)

        def weigh(i, size, totals):
            added = None
            for r in range(size):
                weights = jnp.exp2(scores_ref[i + r] * EXP2_SCALE - shift)
                block = 2 * (pair_low + i + r)
                values_t = jnp.concatenate(
                    [kv_ref[block, SLAB:], kv_ref[block + 1, SLAB:]], axis=1
                )
                part = contract(values_t, weights.astype(jnp.bfloat16), 1, 0)
                added = part if added is None else added + part
                totals = totals + jnp.sum(weights.reshape(PAIR // 8, 8, columns), axis=0)
            acc_ref[...] += added
            return totals

        totals = in_steps(pairs, STEPS, weigh, jnp.zeros((8, columns), jnp.float32))
        totals = jnp.sum(totals, axis=0, keepdims=True)
        attended_t = (acc_ref[...] / totals).astype(jnp.bfloat16)
        back = contract(select, attended_t, 1, 1).astype(jnp.bfloat16)
        out_ref[:, z] = back.reshape(N_DP, Q_ROWS, HEAD_SIZE)
        return carry

    lax.fori_loop(0, N_Z, slab, 0)


def unpack_kernel(targets_ref, slots_ref, out_ref):
    select = one_hot(GROUP_HEADS * SLAB, targets_ref[...])
    for z in range(N_Z):
        slots = slots_ref[:, z].reshape(N_DP * Q_ROWS, HEAD_SIZE)
        rows = contract(select, slots, 1, 0).astype(jnp.bfloat16)
        for h in range(GROUP_HEADS):
            at = (z * GROUP_HEADS + h) * HEAD_SIZE
            out_ref[:, at : at + HEAD_SIZE] = rows[h * SLAB : (h + 1) * SLAB]


def call(kernel, name, outs, specs, flops, moved, exps=0, scratch=(), vmem=VMEM_BYTES):
    return pl.pallas_call(
        kernel,
        name=name,
        out_shape=[jax.ShapeDtypeStruct(shape, dtype) for shape, dtype in outs],
        in_specs=[pl.BlockSpec(memory_space=s) for s in specs],
        out_specs=[pl.BlockSpec(memory_space=pltpu.VMEM)] * len(outs),
        scratch_shapes=scratch,
        compiler_params=pltpu.CompilerParams(vmem_limit_bytes=vmem),
        cost_estimate=pl.CostEstimate(flops=flops, bytes_accessed=moved, transcendentals=exps),
    )


def exchange(blocks):
    flat = blocks.reshape((N_DP * N_Z,) + blocks.shape[2:])
    flat = lax.all_to_all(flat, EXCHANGE, split_axis=0, concat_axis=0, tiled=True)
    return flat.reshape(blocks.shape)


def local(query, key, value, doc_lengths, send_slots, slab_source, back_pack, back_index):
    V, S, H = pltpu.VMEM, pltpu.SMEM, pl.ANY
    half, whole = jnp.bfloat16, jnp.int32
    columns = GROUP_HEADS * SLAB
    q_blocks = (N_DP, N_Z, Q_ROWS, HEAD_SIZE)
    kv_blocks = (N_DP, N_Z, KV_ROWS, HEAD_SIZE)
    (kv_sent,) = call(
        pack_kv_kernel,
        "pack_kv",
        [(kv_blocks, half)],
        [H, H, H, H],
        2 * 10**8,
        2 * 10**6,
        0,
        [
            V((1, 1, SLAB), whole),
            V((1, 1, SLAB), whole),
            V((2 * SLAB, KEY_VALUE_HEADS * HEAD_SIZE), half),
            pltpu.SemaphoreType.DMA((4,)),
        ],
        60 * 1024 * 1024,
    )(back_index, slab_source, key, value)
    kv_slots = exchange(kv_sent)
    own_code = back_index.reshape(1, SLAB)
    (q_sent,) = call(pack_q_kernel, "pack_q", [(q_blocks, half)], [V, V], 8 * 10**8, 3 * 10**6)(
        own_code, query
    )
    q_sent, kv_slots = lax.optimization_barrier((q_sent, kv_slots))
    q_slots = exchange(q_sent)
    group = lax.axis_index(("y", "core")).astype(whole).reshape(1)
    kv_placed, code = call(
        place_kv_kernel,
        "place_kv",
        [((N_Z, 2 * SLAB, HEAD_SIZE), half), ((N_Z, SLAB), whole)],
        [S, V],
        2 * 10**8,
        2 * 10**6,
    )(group, kv_slots)
    lane = lax.axis_index("x").astype(whole).reshape(1)
    pieces = [kv_placed] + [
        lax.ppermute(kv_placed, "x", [(x, (x + back) % N_X) for x in range(N_X)])
        for back in range(1, N_X)
    ]
    (kv_blocks_all,) = call(
        order_kv_kernel,
        "order_kv",
        [((N_Z * N_X, 2 * SLAB, HEAD_SIZE), half)],
        [S] + [V] * N_X,
        10**6,
        4 * 10**6,
    )(lane, *pieces)
    (out_sent,) = call(
        attend_kernel,
        "attend",
        [(q_blocks, half)],
        [S, S, V, V, V],
        4 * 10**9,
        5 * 10**6,
        3 * 10**6,
        [V((MAX_PAIRS, PAIR, columns), jnp.float32), V((HEAD_SIZE, columns), jnp.float32)],
    )(doc_lengths.reshape(DOCS), lane, code, q_slots, kv_blocks_all)
    out_slots = exchange(out_sent)
    sent = send_slots.reshape(N_DP, 1, CAP)
    head = jnp.arange(GROUP_HEADS, dtype=whole).reshape(1, GROUP_HEADS, 1)
    targets = jnp.where(sent < SLAB, sent + head * SLAB, -1).reshape(1, N_DP * Q_ROWS)
    (out,) = call(
        unpack_kernel,
        "unpack",
        [((SLAB, QUERY_HEADS * HEAD_SIZE), half)],
        [V, V],
        8 * 10**8,
        3 * 10**6,
    )(targets, out_slots)
    return out


def solution(mesh):
    wide = Mesh(mesh.devices.reshape(N_DP // 2, 2, N_Z, N_X), ("y", "core", "z", "x"))
    rows = P(("y", "core", "z", "x"), None)
    table = P(("y", "core"), ("z", "x"), None)
    return jax.shard_map(
        local,
        mesh=wide,
        in_specs=(rows, rows, rows, P(("y", "core"), None, None), table, table, table, table),
        out_specs=rows,
        check_vma=False,
    )
```

```python
import math

import jax
import jax.numpy as jnp
from jax import lax
from jax.experimental import pallas as pl
from jax.experimental.pallas import tpu as pltpu
from jax.sharding import Mesh, PartitionSpec as P

QUERY_HEADS = 32
KEY_VALUE_HEADS = 8
HEAD_SIZE = 128
GROUP_HEADS = QUERY_HEADS // KEY_VALUE_HEADS
CAP = 12
N_DP = 16
N_Z = 8
N_X = 4
SLAB = 128
DOCS = 8
MOST = 2048
WIDE = 2 * HEAD_SIZE
HEAD_PAIRS = GROUP_HEADS // 2
Q_ROWS = HEAD_PAIRS * CAP
KV_ROWS = 16
PAIR = 2 * SLAB
PAIR_BITS = 8
MAX_ITEMS = 48
STEPS = (8, 2, 1)
EXP2_SCALE = math.log2(math.e) / math.sqrt(HEAD_SIZE)
MASKED = -1e30
VMEM_BYTES = 24 * 1024 * 1024
EXCHANGE = ("y", "core", "z")


def slot_rows(code, runs, block_rows):
    peer = (code * 171) >> 11
    base = peer * block_rows + (code - peer * CAP)
    return jnp.concatenate([base + run * CAP for run in range(runs)], axis=1)


def one_hot(rows, targets):
    at = lax.broadcasted_iota(jnp.int32, (rows, targets.shape[1]), 0)
    return jnp.where(at == targets, 1.0, 0.0).astype(jnp.bfloat16)


def contract(a, b, dim_a, dim_b):
    return lax.dot_general(
        a, b, (((dim_a,), (dim_b,)), ((), ())), preferred_element_type=jnp.float32
    )


def pack_kv_kernel(
    code_ref, table_ref, key_ref, value_ref, out_ref, code, table, rows, sems
):
    copies = [
        pltpu.make_async_copy(code_ref, code, sems.at[0]),
        pltpu.make_async_copy(table_ref, table, sems.at[1]),
        pltpu.make_async_copy(key_ref, rows.at[:SLAB], sems.at[2]),
        pltpu.make_async_copy(value_ref, rows.at[SLAB:], sems.at[3]),
    ]
    for copy in copies:
        copy.start()
    for copy in copies:
        copy.wait()
    select = one_hot(N_DP * KV_ROWS, slot_rows(code[0], 1, KV_ROWS))
    codes = table[0].astype(jnp.float32)
    at = lax.broadcasted_iota(jnp.int32, (N_DP * KV_ROWS, WIDE), 0) & (KV_ROWS - 1)
    codes = jnp.where(at >= CAP, jnp.concatenate([codes, codes], axis=1), 0.0)
    for z in range(N_Z):
        lanes = slice(z * HEAD_SIZE, (z + 1) * HEAD_SIZE)
        both = jnp.concatenate([rows[:SLAB, lanes], rows[SLAB:, lanes]], axis=1)
        sent = (contract(select, both, 1, 0) + codes).astype(jnp.bfloat16)
        out_ref[:, z] = sent.reshape(N_DP, KV_ROWS, WIDE)


def pack_q_kernel(code_ref, query_ref, out_ref):
    select = one_hot(N_DP * Q_ROWS, slot_rows(code_ref[...], HEAD_PAIRS, Q_ROWS))
    for z in range(N_Z):
        first = z * HEAD_PAIRS
        rows = jnp.concatenate(
            [query_ref[:, (first + p) * WIDE : (first + p + 1) * WIDE] for p in range(HEAD_PAIRS)],
            axis=0,
        )
        sent = contract(select, rows, 1, 0).astype(jnp.bfloat16)
        out_ref[:, z] = sent.reshape(N_DP, Q_ROWS, WIDE)


def place_kv_kernel(group_ref, slots_ref, out_ref, code_ref):
    group = group_ref[0]
    for z in range(N_Z):
        own = slots_ref[group, z].astype(jnp.float32).astype(jnp.int32)
        code = own[CAP : CAP + 1, :SLAB]
        code_ref[z : z + 1, :] = code
        select = one_hot(N_DP * KV_ROWS, slot_rows(code, 1, KV_ROWS))
        slots = slots_ref[:, z].reshape(N_DP * KV_ROWS, WIDE)
        keys = contract(select, slots[:, :HEAD_SIZE], 0, 0)
        values_t = contract(slots[:, HEAD_SIZE:], select, 0, 0)
        out_ref[z, :SLAB] = keys.astype(jnp.bfloat16)
        out_ref[z, SLAB:] = values_t.astype(jnp.bfloat16)


def order_kv_kernel(lane_ref, *refs):
    out_ref = refs[N_X]
    for back, piece_ref in enumerate(refs[:N_X]):
        x = (lane_ref[0] - back) & (N_X - 1)
        for z in range(N_Z):
            out_ref[z * N_X + x] = piece_ref[z]


def each_item(items, end_of, body):
    done, slab = jnp.int32(0), jnp.int32(0)
    for size in STEPS:
        steps = (items - done) // size if size > 1 else items - done

        def step(i, slab, done=done, size=size):
            for r in range(size):
                item = done + i * size + r
                slab = jnp.where(item >= end_of[slab], slab + 1, slab)
                body(item, slab)
            return slab

        slab = lax.fori_loop(0, steps, step, slab)
        done = done + steps * size


def attend_kernel(
    lengths_ref,
    lane_ref,
    code_ref,
    slots_hbm,
    kv_ref,
    out_hbm,
    slots_ref,
    out_ref,
    select_ref,
    query_ref,
    scores_ref,
    tops_ref,
    sums_ref,
    acc_ref,
    low_of,
    end_of,
    in_sems,
    out_sems,
):
    lane = lane_ref[0]
    columns = GROUP_HEADS * SLAB

    def copy_in(z):
        return pltpu.make_async_copy(slots_hbm.at[:, z], slots_ref.at[z], in_sems.at[z])

    def copy_out(z):
        return pltpu.make_async_copy(out_ref.at[z], out_hbm.at[:, z], out_sems.at[z])

    for z in range(N_Z):
        copy_in(z).start()

    bounds = []
    total = jnp.int32(0)
    for i in range(DOCS):
        total = total + lengths_ref[i]
        bounds.append(total)

    items = jnp.int32(0)
    for z in range(N_Z):
        first = (z * N_X + lane) * SLAB
        start = jnp.int32(0)
        for bound in bounds:
            start = jnp.where(first >= bound, bound, start)
        low = start >> PAIR_BITS
        low_of[z] = low - items
        items = items + (first >> PAIR_BITS) - low + 1
        end_of[z] = items

    @pl.loop(0, N_Z)
    def _(z):
        targets = slot_rows(code_ref[pl.ds(z, 1), :], HEAD_PAIRS, Q_ROWS)
        select_ref[z] = one_hot(N_DP * Q_ROWS, targets)
        tops_ref[z] = jnp.full((8, columns), MASKED, jnp.float32)
        sums_ref[z] = jnp.zeros((8, columns), jnp.float32)
        acc_ref[z] = jnp.zeros((HEAD_SIZE, columns), jnp.float32)
        copy_in(z).wait()
        slots = slots_ref[z].reshape(N_DP * Q_ROWS, WIDE)
        query_t = contract(slots, select_ref[z], 0, 0).astype(jnp.bfloat16)
        query_ref[z, :, : columns // 2] = query_t[:HEAD_SIZE]
        query_ref[z, :, columns // 2 :] = query_t[HEAD_SIZE:]

    in_slab = lax.broadcasted_iota(jnp.int32, (1, SLAB), 1)
    in_pair = lax.broadcasted_iota(jnp.int32, (PAIR, SLAB), 0)

    def score(item, z):
        pair = low_of[z] + item
        query_at = (z * N_X + lane) * SLAB + in_slab
        start = jnp.zeros((1, SLAB), jnp.int32)
        for bound in bounds:
            start = jnp.where(query_at >= bound, bound, start)
        at = pair * PAIR
        allowed = (in_pair >= start - at) & (in_pair <= query_at - at)
        keys = jnp.concatenate([kv_ref[2 * pair, :SLAB], kv_ref[2 * pair + 1, :SLAB]], axis=0)
        s = contract(keys, query_ref[z], 1, 0)
        tops = []
        for h in range(GROUP_HEADS):
            lanes = slice(h * SLAB, (h + 1) * SLAB)
            masked = jnp.where(allowed, s[:, lanes], MASKED)
            scores_ref[item, :, lanes] = masked
            tops.append(jnp.max(masked.reshape(PAIR // 8, 8, SLAB), axis=0))
        tops_ref[z] = jnp.maximum(tops_ref[z], jnp.concatenate(tops, axis=1))

    each_item(items, end_of, score)

    @pl.loop(0, N_Z)
    def _(z):
        shift = jnp.max(tops_ref[z], axis=0, keepdims=True) * EXP2_SCALE
        tops_ref[z] = jnp.broadcast_to(shift, (8, columns))

    def weigh(item, z):
        pair = low_of[z] + item
        weights = jnp.exp2(scores_ref[item] * EXP2_SCALE - tops_ref[z, :1])
        values_t = jnp.concatenate([kv_ref[2 * pair, SLAB:], kv_ref[2 * pair + 1, SLAB:]], axis=1)
        acc_ref[z] += contract(values_t, weights.astype(jnp.bfloat16), 1, 0)
        sums_ref[z] += jnp.sum(weights.reshape(PAIR // 8, 8, columns), axis=0)

    each_item(items, end_of, weigh)

    @pl.loop(0, N_Z)
    def _(z):
        totals = jnp.sum(sums_ref[z], axis=0, keepdims=True)
        attended_t = (acc_ref[z] * (1.0 / totals)).astype(jnp.bfloat16)
        attended_t = jnp.concatenate(
            [attended_t[:, : columns // 2], attended_t[:, columns // 2 :]], axis=0
        )
        back = contract(select_ref[z], attended_t, 1, 1).astype(jnp.bfloat16)
        out_ref[z] = back.reshape(N_DP, Q_ROWS, WIDE)
        copy_out(z).start()

    @pl.loop(0, N_Z)
    def _(z):
        copy_out(z).wait()


def unpack_kernel(targets_ref, slots_ref, out_ref):
    select = one_hot(HEAD_PAIRS * SLAB, targets_ref[...])
    for z in range(N_Z):
        slots = slots_ref[:, z].reshape(N_DP * Q_ROWS, WIDE)
        rows = contract(select, slots, 1, 0).astype(jnp.bfloat16)
        for p in range(HEAD_PAIRS):
            at = (z * HEAD_PAIRS + p) * WIDE
            out_ref[:, at : at + WIDE] = rows[p * SLAB : (p + 1) * SLAB]


def call(kernel, name, outs, specs, flops, moved, exps=0, scratch=(), vmem=VMEM_BYTES, out_space=pltpu.VMEM):
    return pl.pallas_call(
        kernel,
        name=name,
        out_shape=[jax.ShapeDtypeStruct(shape, dtype) for shape, dtype in outs],
        in_specs=[pl.BlockSpec(memory_space=s) for s in specs],
        out_specs=[pl.BlockSpec(memory_space=out_space)] * len(outs),
        scratch_shapes=scratch,
        compiler_params=pltpu.CompilerParams(vmem_limit_bytes=vmem),
        cost_estimate=pl.CostEstimate(flops=flops, bytes_accessed=moved, transcendentals=exps),
    )


def exchange(blocks):
    flat = blocks.reshape((N_DP * N_Z,) + blocks.shape[2:])
    flat = lax.all_to_all(flat, EXCHANGE, split_axis=0, concat_axis=0, tiled=True)
    return flat.reshape(blocks.shape)


def local(query, key, value, doc_lengths, send_slots, slab_source, back_pack, back_index):
    V, S, H = pltpu.VMEM, pltpu.SMEM, pl.ANY
    half, whole = jnp.bfloat16, jnp.int32
    columns = GROUP_HEADS * SLAB
    q_blocks = (N_DP, N_Z, Q_ROWS, WIDE)
    kv_blocks = (N_DP, N_Z, KV_ROWS, WIDE)
    (kv_sent,) = call(
        pack_kv_kernel,
        "pack_kv",
        [(kv_blocks, half)],
        [H, H, H, H],
        2 * 10**8,
        2 * 10**6,
        0,
        [
            V((1, 1, SLAB), whole),
            V((1, 1, SLAB), whole),
            V((2 * SLAB, KEY_VALUE_HEADS * HEAD_SIZE), half),
            pltpu.SemaphoreType.DMA((4,)),
        ],
        60 * 1024 * 1024,
    )(back_index, slab_source, key, value)
    kv_slots = exchange(kv_sent)
    own_code = back_index.reshape(1, SLAB)
    (q_sent,) = call(pack_q_kernel, "pack_q", [(q_blocks, half)], [V, V], 8 * 10**8, 3 * 10**6)(
        own_code, query
    )
    sent = send_slots.reshape(N_DP, 1, CAP)
    run = jnp.arange(HEAD_PAIRS, dtype=whole).reshape(1, HEAD_PAIRS, 1)
    targets = jnp.where(sent < SLAB, sent + run * SLAB, -1).reshape(1, N_DP * Q_ROWS)
    q_sent, kv_slots, targets = lax.optimization_barrier((q_sent, kv_slots, targets))
    q_slots = exchange(q_sent)
    group = lax.axis_index(("y", "core")).astype(whole).reshape(1)
    kv_placed, code = call(
        place_kv_kernel,
        "place_kv",
        [((N_Z, 2 * SLAB, HEAD_SIZE), half), ((N_Z, SLAB), whole)],
        [S, V],
        2 * 10**8,
        2 * 10**6,
    )(group, kv_slots)
    lane = lax.axis_index("x").astype(whole).reshape(1)
    pieces = [kv_placed] + [
        lax.ppermute(kv_placed, "x", [(x, (x + back) % N_X) for x in range(N_X)])
        for back in range(1, N_X)
    ]
    (kv_blocks_all,) = call(
        order_kv_kernel,
        "order_kv",
        [((N_Z * N_X, 2 * SLAB, HEAD_SIZE), half)],
        [S] + [V] * N_X,
        10**6,
        4 * 10**6,
    )(lane, *pieces)
    f32 = jnp.float32
    (out_sent,) = call(
        attend_kernel,
        "attend",
        [(q_blocks, half)],
        [S, S, V, pl.ANY, V],
        4 * 10**9,
        5 * 10**6,
        3 * 10**6,
        [
            V((N_Z, N_DP, Q_ROWS, WIDE), half),
            V((N_Z, N_DP, Q_ROWS, WIDE), half),
            V((N_Z, N_DP * Q_ROWS, HEAD_PAIRS * SLAB), half),
            V((N_Z, HEAD_SIZE, columns), half),
            V((MAX_ITEMS, PAIR, columns), f32),
            V((N_Z, 8, columns), f32),
            V((N_Z, 8, columns), f32),
            V((N_Z, HEAD_SIZE, columns), f32),
            S((N_Z,), whole),
            S((N_Z,), whole),
            pltpu.SemaphoreType.DMA((N_Z,)),
            pltpu.SemaphoreType.DMA((N_Z,)),
        ],
        48 * 1024 * 1024,
        pl.ANY,
    )(doc_lengths.reshape(DOCS), lane, code, q_slots, kv_blocks_all)
    out_slots = exchange(out_sent)
    (out,) = call(
        unpack_kernel,
        "unpack",
        [((SLAB, QUERY_HEADS * HEAD_SIZE), half)],
        [V, V],
        8 * 10**8,
        3 * 10**6,
    )(targets, out_slots)
    return out


def solution(mesh):
    wide = Mesh(mesh.devices.reshape(N_DP // 2, 2, N_Z, N_X), ("y", "core", "z", "x"))
    rows = P(("y", "core", "z", "x"), None)
    table = P(("y", "core"), ("z", "x"), None)
    return jax.shard_map(
        local,
        mesh=wide,
        in_specs=(rows, rows, rows, P(("y", "core"), None, None), table, table, table, table),
        out_specs=rows,
        check_vma=False,
    )
```

```python
import math

import jax
import jax.numpy as jnp
from jax import lax
from jax.experimental import pallas as pl
from jax.experimental.pallas import tpu as pltpu
from jax.sharding import Mesh, PartitionSpec as P

QUERY_HEADS = 32
KEY_VALUE_HEADS = 8
HEAD_SIZE = 128
GROUP_HEADS = QUERY_HEADS // KEY_VALUE_HEADS
CAP = 12
N_DP = 16
N_Z = 8
N_X = 4
SLAB = 128
DOCS = 8
MOST = 2048
WIDE = 2 * HEAD_SIZE
HEAD_PAIRS = GROUP_HEADS // 2
Q_ROWS = HEAD_PAIRS * CAP
KV_ROWS = 16
PAIR = 2 * SLAB
SLAB_BITS = 7
MAX_ITEMS = 48
STEPS = (8, 2, 1)
EXP2_SCALE = math.log2(math.e) / math.sqrt(HEAD_SIZE)
MASKED = -1e30
VMEM_BYTES = 16 * 1024 * 1024
EXCHANGE = ("y", "core", "z")


def slot_rows(code, runs, block_rows):
    peer = (code * 171) >> 11
    base = peer * block_rows + (code - peer * CAP)
    return jnp.concatenate([base + run * CAP for run in range(runs)], axis=1)


def one_hot(rows, targets):
    at = lax.broadcasted_iota(jnp.int32, (rows, targets.shape[1]), 0)
    return jnp.where(at == targets, 1.0, 0.0).astype(jnp.bfloat16)


def contract(a, b, dim_a, dim_b):
    return lax.dot_general(
        a, b, (((dim_a,), (dim_b,)), ((), ())), preferred_element_type=jnp.float32
    )


def copy_slab(slabs_ref, blocks_hbm, sems, z):
    return pltpu.make_async_copy(slabs_ref.at[z], blocks_hbm.at[:, z], sems.at[z])


def pack_kv_kernel(
    code_ref, table_ref, key_ref, value_ref, out_hbm, code, table, rows, out_ref, sems, out_sems
):
    copies = [
        pltpu.make_async_copy(code_ref, code, sems.at[0]),
        pltpu.make_async_copy(table_ref, table, sems.at[1]),
        pltpu.make_async_copy(key_ref, rows.at[:SLAB], sems.at[2]),
        pltpu.make_async_copy(value_ref, rows.at[SLAB:], sems.at[3]),
    ]
    for copy in copies:
        copy.start()
    for copy in copies:
        copy.wait()
    select = one_hot(N_DP * KV_ROWS, slot_rows(code[0], 1, KV_ROWS))
    codes = table[0].astype(jnp.float32)
    at = lax.broadcasted_iota(jnp.int32, (N_DP * KV_ROWS, WIDE), 0) & (KV_ROWS - 1)
    codes = jnp.where(at >= CAP, jnp.concatenate([codes, codes], axis=1), 0.0)
    for z in range(N_Z):
        lanes = slice(z * HEAD_SIZE, (z + 1) * HEAD_SIZE)
        both = jnp.concatenate([rows[:SLAB, lanes], rows[SLAB:, lanes]], axis=1)
        sent = (contract(select, both, 1, 0) + codes).astype(jnp.bfloat16)
        out_ref[z] = sent.reshape(N_DP, KV_ROWS, WIDE)
        copy_slab(out_ref, out_hbm, out_sems, z).start()
    for z in range(N_Z):
        copy_slab(out_ref, out_hbm, out_sems, z).wait()


def pack_q_kernel(code_ref, query_ref, out_ref):
    select = one_hot(N_DP * Q_ROWS, slot_rows(code_ref[...], HEAD_PAIRS, Q_ROWS))
    for z in range(N_Z):
        first = z * HEAD_PAIRS
        rows = jnp.concatenate(
            [query_ref[:, (first + p) * WIDE : (first + p + 1) * WIDE] for p in range(HEAD_PAIRS)],
            axis=0,
        )
        sent = contract(select, rows, 1, 0).astype(jnp.bfloat16)
        out_ref[:, z] = sent.reshape(N_DP, Q_ROWS, WIDE)


def place_kv_kernel(group_ref, slots_ref, out_ref, code_ref):
    group = group_ref[0]
    for z in range(N_Z):
        own = slots_ref[group, z].astype(jnp.float32).astype(jnp.int32)
        code = own[CAP : CAP + 1, :SLAB]
        code_ref[z : z + 1, :] = code
        select = one_hot(N_DP * KV_ROWS, slot_rows(code, 1, KV_ROWS))
        slots = slots_ref[:, z].reshape(N_DP * KV_ROWS, WIDE)
        keys = contract(select, slots[:, :HEAD_SIZE], 0, 0)
        values_t = contract(slots[:, HEAD_SIZE:], select, 0, 0)
        out_ref[z, :SLAB] = keys.astype(jnp.bfloat16)
        out_ref[z, SLAB:] = values_t.astype(jnp.bfloat16)


def each_item(items, end_of, body):
    done, slab = jnp.int32(0), jnp.int32(0)
    for size in STEPS:
        steps = (items - done) // size if size > 1 else items - done

        def step(i, slab, done=done, size=size):
            for r in range(size):
                item = done + i * size + r
                slab = jnp.where(item >= end_of[slab], slab + 1, slab)
                body(item, slab)
            return slab

        slab = lax.fori_loop(0, steps, step, slab)
        done = done + steps * size


def attend_kernel(
    lengths_ref,
    lane_ref,
    code_ref,
    slots_hbm,
    piece_0,
    piece_1,
    piece_2,
    piece_3,
    out_hbm,
    kv_ref,
    slots_ref,
    out_ref,
    select_ref,
    query_ref,
    scores_ref,
    tops_ref,
    sums_ref,
    acc_ref,
    low_of,
    end_of,
    in_sems,
    out_sems,
    piece_sems,
):
    lane = lane_ref[0]
    columns = GROUP_HEADS * SLAB

    def copy_in(z):
        return pltpu.make_async_copy(slots_hbm.at[:, z], slots_ref.at[z], in_sems.at[z])

    pieces = [
        pltpu.make_async_copy(piece, kv_ref.at[:, (lane - back) & (N_X - 1)], piece_sems.at[back])
        for back, piece in enumerate((piece_0, piece_1, piece_2, piece_3))
    ]

    for z in range(N_Z):
        copy_in(z).start()
    for piece in pieces:
        piece.start()

    bounds = []
    total = jnp.int32(0)
    for i in range(DOCS):
        total = total + lengths_ref[i]
        bounds.append(total)

    items = jnp.int32(0)
    for z in range(N_Z):
        first = (z * N_X + lane) * SLAB
        start = jnp.int32(0)
        for bound in bounds:
            start = jnp.where(first >= bound, bound, start)
        block = z * N_X + lane
        count = (block - (start >> SLAB_BITS) + 2) >> 1
        low_of[z] = block + 1 - 2 * count - 2 * items
        items = items + count
        end_of[z] = items

    @pl.loop(0, N_Z)
    def _(z):
        targets = slot_rows(code_ref[pl.ds(z, 1), :], HEAD_PAIRS, Q_ROWS)
        select_ref[z] = one_hot(N_DP * Q_ROWS, targets)
        tops_ref[z] = jnp.full((8, columns), MASKED, jnp.float32)
        sums_ref[z] = jnp.zeros((8, columns), jnp.float32)
        acc_ref[z] = jnp.zeros((HEAD_SIZE, columns), jnp.float32)
        copy_in(z).wait()
        slots = slots_ref[z].reshape(N_DP * Q_ROWS, WIDE)
        query_t = contract(slots, select_ref[z], 0, 0).astype(jnp.bfloat16)
        query_ref[z, :, : columns // 2] = query_t[:HEAD_SIZE]
        query_ref[z, :, columns // 2 :] = query_t[HEAD_SIZE:]

    for piece in pieces:
        piece.wait()

    def place(item, z):
        block = low_of[z] + 2 * item
        lower = jnp.maximum(block, 0)
        return block, (lower >> 2, lower & 3), ((block + 1) >> 2, (block + 1) & 3)

    in_slab = lax.broadcasted_iota(jnp.int32, (1, SLAB), 1)
    in_pair = lax.broadcasted_iota(jnp.int32, (PAIR, SLAB), 0)

    def score(item, z):
        block, one, two = place(item, z)
        query_at = (z * N_X + lane) * SLAB + in_slab
        start = jnp.zeros((1, SLAB), jnp.int32)
        for bound in bounds:
            start = jnp.where(query_at >= bound, bound, start)
        at = block * SLAB
        allowed = (in_pair >= start - at) & (in_pair <= query_at - at)
        keys = jnp.concatenate([kv_ref[*one, :SLAB], kv_ref[*two, :SLAB]], axis=0)
        s = contract(keys, query_ref[z], 1, 0) * EXP2_SCALE
        tops = []
        for h in range(GROUP_HEADS):
            lanes = slice(h * SLAB, (h + 1) * SLAB)
            masked = jnp.where(allowed, s[:, lanes], MASKED)
            scores_ref[item, :, lanes] = masked
            tops.append(jnp.max(masked.reshape(PAIR // 8, 8, SLAB), axis=0))
        tops_ref[z] = jnp.maximum(tops_ref[z], jnp.concatenate(tops, axis=1))

    each_item(items, end_of, score)

    @pl.loop(0, N_Z)
    def _(z):
        shift = jnp.max(tops_ref[z], axis=0, keepdims=True)
        tops_ref[z] = jnp.broadcast_to(shift, (8, columns))

    def weigh(item, z):
        _, one, two = place(item, z)
        weights = jnp.exp2(scores_ref[item] - tops_ref[z, :1])
        values_t = jnp.concatenate([kv_ref[*one, SLAB:], kv_ref[*two, SLAB:]], axis=1)
        acc_ref[z] += contract(values_t, weights.astype(jnp.bfloat16), 1, 0)
        sums_ref[z] += jnp.sum(weights.reshape(PAIR // 8, 8, columns), axis=0)

    each_item(items, end_of, weigh)

    @pl.loop(0, N_Z)
    def _(z):
        totals = jnp.sum(sums_ref[z], axis=0, keepdims=True)
        attended_t = (acc_ref[z] * (1.0 / totals)).astype(jnp.bfloat16)
        attended_t = jnp.concatenate(
            [attended_t[:, : columns // 2], attended_t[:, columns // 2 :]], axis=0
        )
        back = contract(select_ref[z], attended_t, 1, 1).astype(jnp.bfloat16)
        out_ref[z] = back.reshape(N_DP, Q_ROWS, WIDE)
        copy_slab(out_ref, out_hbm, out_sems, z).start()

    @pl.loop(0, N_Z)
    def _(z):
        copy_slab(out_ref, out_hbm, out_sems, z).wait()


def unpack_kernel(targets_ref, slots_ref, out_hbm, out_ref, sems):
    def copy_out(z):
        lanes = pl.ds(z * HEAD_PAIRS * WIDE, HEAD_PAIRS * WIDE)
        return pltpu.make_async_copy(out_ref.at[z], out_hbm.at[:, lanes], sems.at[z])

    select = one_hot(HEAD_PAIRS * SLAB, targets_ref[...])
    for z in range(N_Z):
        slots = slots_ref[:, z].reshape(N_DP * Q_ROWS, WIDE)
        rows = contract(select, slots, 1, 0).astype(jnp.bfloat16)
        for p in range(HEAD_PAIRS):
            out_ref[z, :, p * WIDE : (p + 1) * WIDE] = rows[p * SLAB : (p + 1) * SLAB]
        copy_out(z).start()
    for z in range(N_Z):
        copy_out(z).wait()


def call(kernel, name, outs, specs, flops, moved, exps=0, scratch=(), vmem=VMEM_BYTES, out_space=pltpu.VMEM):
    return pl.pallas_call(
        kernel,
        name=name,
        out_shape=[jax.ShapeDtypeStruct(shape, dtype) for shape, dtype in outs],
        in_specs=[pl.BlockSpec(memory_space=s) for s in specs],
        out_specs=[pl.BlockSpec(memory_space=out_space)] * len(outs),
        scratch_shapes=scratch,
        compiler_params=pltpu.CompilerParams(vmem_limit_bytes=vmem),
        cost_estimate=pl.CostEstimate(flops=flops, bytes_accessed=moved, transcendentals=exps),
    )


def exchange(blocks):
    flat = blocks.reshape((N_DP * N_Z,) + blocks.shape[2:])
    flat = lax.all_to_all(flat, EXCHANGE, split_axis=0, concat_axis=0, tiled=True)
    return flat.reshape(blocks.shape)


def local(query, key, value, doc_lengths, send_slots, slab_source, back_pack, back_index):
    V, S, H = pltpu.VMEM, pltpu.SMEM, pl.ANY
    half, whole = jnp.bfloat16, jnp.int32
    columns = GROUP_HEADS * SLAB
    q_blocks = (N_DP, N_Z, Q_ROWS, WIDE)
    kv_blocks = (N_DP, N_Z, KV_ROWS, WIDE)
    (kv_sent,) = call(
        pack_kv_kernel,
        "pack_kv",
        [(kv_blocks, half)],
        [H, H, H, H],
        2 * 10**8,
        2 * 10**6,
        0,
        [
            V((1, 1, SLAB), whole),
            V((1, 1, SLAB), whole),
            V((2 * SLAB, KEY_VALUE_HEADS * HEAD_SIZE), half),
            V((N_Z, N_DP, KV_ROWS, WIDE), half),
            pltpu.SemaphoreType.DMA((4,)),
            pltpu.SemaphoreType.DMA((N_Z,)),
        ],
        60 * 1024 * 1024,
        pl.ANY,
    )(back_index, slab_source, key, value)
    kv_slots = exchange(kv_sent)
    own_code = back_index.reshape(1, SLAB)
    (q_sent,) = call(pack_q_kernel, "pack_q", [(q_blocks, half)], [V, V], 8 * 10**8, 3 * 10**6)(
        own_code, query
    )
    sent = send_slots.reshape(N_DP, 1, CAP)
    run = jnp.arange(HEAD_PAIRS, dtype=whole).reshape(1, HEAD_PAIRS, 1)
    targets = jnp.where(sent < SLAB, sent + run * SLAB, -1).reshape(1, N_DP * Q_ROWS)
    q_sent, kv_slots, targets = lax.optimization_barrier((q_sent, kv_slots, targets))
    q_slots = exchange(q_sent)
    group = lax.axis_index(("y", "core")).astype(whole).reshape(1)
    kv_placed, code = call(
        place_kv_kernel,
        "place_kv",
        [((N_Z, 2 * SLAB, HEAD_SIZE), half), ((N_Z, SLAB), whole)],
        [S, V],
        2 * 10**8,
        2 * 10**6,
    )(group, kv_slots)
    lane = lax.axis_index("x").astype(whole).reshape(1)
    pieces = [kv_placed] + [
        lax.ppermute(kv_placed, "x", [(x, (x + back) % N_X) for x in range(N_X)])
        for back in range(1, N_X)
    ]
    f32 = jnp.float32
    (out_sent,) = call(
        attend_kernel,
        "attend",
        [(q_blocks, half)],
        [S, S, V] + [pl.ANY] * (1 + N_X),
        4 * 10**9,
        5 * 10**6,
        3 * 10**6,
        [
            V((N_Z, N_X, 2 * SLAB, HEAD_SIZE), half),
            V((N_Z, N_DP, Q_ROWS, WIDE), half),
            V((N_Z, N_DP, Q_ROWS, WIDE), half),
            V((N_Z, N_DP * Q_ROWS, HEAD_PAIRS * SLAB), half),
            V((N_Z, HEAD_SIZE, columns), half),
            V((MAX_ITEMS, PAIR, columns), f32),
            V((N_Z, 8, columns), f32),
            V((N_Z, 8, columns), f32),
            V((N_Z, HEAD_SIZE, columns), f32),
            S((N_Z,), whole),
            S((N_Z,), whole),
            pltpu.SemaphoreType.DMA((N_Z,)),
            pltpu.SemaphoreType.DMA((N_Z,)),
            pltpu.SemaphoreType.DMA((N_X,)),
        ],
        40 * 1024 * 1024,
        pl.ANY,
    )(doc_lengths.reshape(DOCS), lane, code, q_slots, *pieces)
    out_slots = exchange(out_sent)
    (out,) = call(
        unpack_kernel,
        "unpack",
        [((SLAB, QUERY_HEADS * HEAD_SIZE), half)],
        [V, V],
        8 * 10**8,
        3 * 10**6,
        0,
        [V((N_Z, SLAB, HEAD_PAIRS * WIDE), half), pltpu.SemaphoreType.DMA((N_Z,))],
        VMEM_BYTES,
        pl.ANY,
    )(targets, out_slots)
    return out


def solution(mesh):
    wide = Mesh(mesh.devices.reshape(N_DP // 2, 2, N_Z, N_X), ("y", "core", "z", "x"))
    rows = P(("y", "core", "z", "x"), None)
    table = P(("y", "core"), ("z", "x"), None)
    return jax.shard_map(
        local,
        mesh=wide,
        in_specs=(rows, rows, rows, P(("y", "core"), None, None), table, table, table, table),
        out_specs=rows,
        check_vma=False,
    )
```

```python
import math

import jax
import jax.numpy as jnp
from jax import lax
from jax.experimental import pallas as pl
from jax.experimental.pallas import tpu as pltpu
from jax.sharding import Mesh, PartitionSpec as P

QUERY_HEADS = 32
KEY_VALUE_HEADS = 8
HEAD_SIZE = 128
GROUP_HEADS = QUERY_HEADS // KEY_VALUE_HEADS
CAP = 12
N_DP = 16
N_Z = 8
N_X = 4
SLAB = 128
DOCS = 8
MOST = 2048
WIDE = 2 * HEAD_SIZE
HEAD_PAIRS = GROUP_HEADS // 2
Q_ROWS = HEAD_PAIRS * CAP
KV_ROWS = 16
PAIR = 2 * SLAB
SLAB_BITS = 7
MAX_ITEMS = 48
STEPS = (16, 8, 4, 2, 1)
EXP2_SCALE = math.log2(math.e) / math.sqrt(HEAD_SIZE)
MASKED = -1e30
VMEM_BYTES = 16 * 1024 * 1024
EXCHANGE = ("y", "core", "z")


def slot_rows(code, runs, block_rows):
    peer = (code * 171) >> 11
    base = peer * block_rows + (code - peer * CAP)
    return jnp.concatenate([base + run * CAP for run in range(runs)], axis=1)


def one_hot(rows, targets):
    at = lax.broadcasted_iota(jnp.int32, (rows, targets.shape[1]), 0)
    return jnp.where(at == targets, 1.0, 0.0).astype(jnp.bfloat16)


def contract(a, b, dim_a, dim_b):
    return lax.dot_general(
        a, b, (((dim_a,), (dim_b,)), ((), ())), preferred_element_type=jnp.float32
    )


def copy_slab(slabs_ref, blocks_hbm, sems, z):
    return pltpu.make_async_copy(slabs_ref.at[z], blocks_hbm.at[:, z], sems.at[z])


def pack_kv_kernel(
    code_ref, table_ref, key_ref, value_ref, out_hbm, code, table, rows, out_ref, sems, out_sems
):
    copies = [
        pltpu.make_async_copy(code_ref, code, sems.at[0]),
        pltpu.make_async_copy(table_ref, table, sems.at[1]),
        pltpu.make_async_copy(key_ref, rows.at[:SLAB], sems.at[2]),
        pltpu.make_async_copy(value_ref, rows.at[SLAB:], sems.at[3]),
    ]
    for copy in copies:
        copy.start()
    for copy in copies[:2]:
        copy.wait()
    select = one_hot(N_DP * KV_ROWS, slot_rows(code[0], 1, KV_ROWS))
    codes = table[0].astype(jnp.float32)
    at = lax.broadcasted_iota(jnp.int32, (N_DP * KV_ROWS, WIDE), 0) & (KV_ROWS - 1)
    codes = jnp.where(at >= CAP, jnp.concatenate([codes, codes], axis=1), 0.0)
    for copy in copies[2:]:
        copy.wait()
    for z in range(N_Z):
        lanes = slice(z * HEAD_SIZE, (z + 1) * HEAD_SIZE)
        both = jnp.concatenate([rows[:SLAB, lanes], rows[SLAB:, lanes]], axis=1)
        sent = (contract(select, both, 1, 0) + codes).astype(jnp.bfloat16)
        out_ref[z] = sent.reshape(N_DP, KV_ROWS, WIDE)
        copy_slab(out_ref, out_hbm, out_sems, z).start()
    for z in range(N_Z):
        copy_slab(out_ref, out_hbm, out_sems, z).wait()


def pack_q_kernel(code_ref, query_ref, out_ref):
    select = one_hot(N_DP * Q_ROWS, slot_rows(code_ref[...], HEAD_PAIRS, Q_ROWS))
    for z in range(N_Z):
        first = z * HEAD_PAIRS
        rows = jnp.concatenate(
            [query_ref[:, (first + p) * WIDE : (first + p + 1) * WIDE] for p in range(HEAD_PAIRS)],
            axis=0,
        )
        sent = contract(select, rows, 1, 0).astype(jnp.bfloat16)
        out_ref[:, z] = sent.reshape(N_DP, Q_ROWS, WIDE)


def place_kv_kernel(group_ref, slots_ref, out_ref, code_ref):
    group = group_ref[0]
    for z in range(N_Z):
        own = slots_ref[group, z].astype(jnp.float32).astype(jnp.int32)
        code = own[CAP : CAP + 1, :SLAB]
        code_ref[z : z + 1, :] = code
        select = one_hot(N_DP * KV_ROWS, slot_rows(code, 1, KV_ROWS))
        slots = slots_ref[:, z].reshape(N_DP * KV_ROWS, WIDE)
        keys = contract(select, slots[:, :HEAD_SIZE], 0, 0)
        values_t = contract(slots[:, HEAD_SIZE:], select, 0, 0)
        out_ref[z, :SLAB] = keys.astype(jnp.bfloat16)
        out_ref[z, SLAB:] = values_t.astype(jnp.bfloat16)


def each_item(items, end_of, body):
    done, slab = jnp.int32(0), jnp.int32(0)
    for size in STEPS:
        steps = (items - done) // size if size > 1 else items - done

        def step(i, slab, done=done, size=size):
            for r in range(size):
                item = done + i * size + r
                slab = jnp.where(item >= end_of[slab], slab + 1, slab)
                body(item, slab)
            return slab

        slab = lax.fori_loop(0, steps, step, slab)
        done = done + steps * size


def attend_kernel(
    lengths_ref,
    lane_ref,
    code_ref,
    slots_hbm,
    piece_0,
    piece_1,
    piece_2,
    piece_3,
    out_hbm,
    kv_ref,
    slots_ref,
    out_ref,
    select_ref,
    query_ref,
    scores_ref,
    tops_ref,
    sums_ref,
    acc_ref,
    low_of,
    end_of,
    in_sems,
    out_sems,
    piece_sems,
):
    lane = lane_ref[0]
    columns = GROUP_HEADS * SLAB

    def copy_in(z):
        return pltpu.make_async_copy(slots_hbm.at[:, z], slots_ref.at[z], in_sems.at[z])

    pieces = [
        pltpu.make_async_copy(piece, kv_ref.at[:, (lane - back) & (N_X - 1)], piece_sems.at[back])
        for back, piece in enumerate((piece_0, piece_1, piece_2, piece_3))
    ]

    for z in range(N_Z):
        copy_in(z).start()
    for piece in pieces:
        piece.start()

    bounds = []
    total = jnp.int32(0)
    for i in range(DOCS):
        total = total + lengths_ref[i]
        bounds.append(total)

    items = jnp.int32(0)
    for z in range(N_Z):
        first = (z * N_X + lane) * SLAB
        start = jnp.int32(0)
        for bound in bounds:
            start = jnp.where(first >= bound, bound, start)
        block = z * N_X + lane
        count = (block - (start >> SLAB_BITS) + 2) >> 1
        low_of[z] = block + 1 - 2 * count - 2 * items
        items = items + count
        end_of[z] = items

    @pl.loop(0, N_Z)
    def _(z):
        targets = slot_rows(code_ref[pl.ds(z, 1), :], HEAD_PAIRS, Q_ROWS)
        select_ref[z] = one_hot(N_DP * Q_ROWS, targets)
        tops_ref[z] = jnp.full((8, columns), MASKED, jnp.float32)
        sums_ref[z] = jnp.zeros((8, columns), jnp.float32)
        acc_ref[z] = jnp.zeros((HEAD_SIZE, columns), jnp.float32)
        copy_in(z).wait()
        slots = slots_ref[z].reshape(N_DP * Q_ROWS, WIDE)
        query_t = contract(slots, select_ref[z], 0, 0).astype(jnp.bfloat16)
        query_ref[z, :, : columns // 2] = query_t[:HEAD_SIZE]
        query_ref[z, :, columns // 2 :] = query_t[HEAD_SIZE:]

    for piece in pieces:
        piece.wait()

    def place(item, z):
        block = low_of[z] + 2 * item
        lower = jnp.maximum(block, 0)
        return block, (lower >> 2, lower & 3), ((block + 1) >> 2, (block + 1) & 3)

    in_slab = lax.broadcasted_iota(jnp.int32, (1, SLAB), 1)
    in_pair = lax.broadcasted_iota(jnp.int32, (PAIR, SLAB), 0)

    def score(item, z):
        block, one, two = place(item, z)
        query_at = (z * N_X + lane) * SLAB + in_slab
        start = jnp.zeros((1, SLAB), jnp.int32)
        for bound in bounds:
            start = jnp.where(query_at >= bound, bound, start)
        at = block * SLAB
        allowed = (in_pair >= start - at) & (in_pair <= query_at - at)
        keys = jnp.concatenate([kv_ref[*one, :SLAB], kv_ref[*two, :SLAB]], axis=0)
        s = contract(keys, query_ref[z], 1, 0) * EXP2_SCALE
        tops = []
        for h in range(GROUP_HEADS):
            lanes = slice(h * SLAB, (h + 1) * SLAB)
            masked = jnp.where(allowed, s[:, lanes], MASKED)
            scores_ref[item, :, lanes] = masked
            tops.append(jnp.max(masked.reshape(PAIR // 8, 8, SLAB), axis=0))
        tops_ref[z] = jnp.maximum(tops_ref[z], jnp.concatenate(tops, axis=1))

    each_item(items, end_of, score)

    @pl.loop(0, N_Z)
    def _(z):
        shift = jnp.max(tops_ref[z], axis=0, keepdims=True)
        tops_ref[z] = jnp.broadcast_to(shift, (8, columns))

    def weigh(item, z):
        _, one, two = place(item, z)
        weights = jnp.exp2(scores_ref[item] - tops_ref[z, :1])
        values_t = jnp.concatenate([kv_ref[*one, SLAB:], kv_ref[*two, SLAB:]], axis=1)
        acc_ref[z] += contract(values_t, weights.astype(jnp.bfloat16), 1, 0)
        sums_ref[z] += jnp.sum(weights.reshape(PAIR // 8, 8, columns), axis=0)

    each_item(items, end_of, weigh)

    @pl.loop(0, N_Z)
    def _(z):
        totals = jnp.sum(sums_ref[z], axis=0, keepdims=True)
        attended_t = (acc_ref[z] * (1.0 / totals)).astype(jnp.bfloat16)
        attended_t = jnp.concatenate(
            [attended_t[:, : columns // 2], attended_t[:, columns // 2 :]], axis=0
        )
        back = contract(select_ref[z], attended_t, 1, 1).astype(jnp.bfloat16)
        out_ref[z] = back.reshape(N_DP, Q_ROWS, WIDE)
        copy_slab(out_ref, out_hbm, out_sems, z).start()

    @pl.loop(0, N_Z)
    def _(z):
        copy_slab(out_ref, out_hbm, out_sems, z).wait()


def unpack_kernel(targets_ref, slots_ref, out_hbm, out_ref, sems):
    def copy_out(z):
        lanes = pl.ds(z * HEAD_PAIRS * WIDE, HEAD_PAIRS * WIDE)
        return pltpu.make_async_copy(out_ref.at[z], out_hbm.at[:, lanes], sems.at[z])

    select = one_hot(HEAD_PAIRS * SLAB, targets_ref[...])
    for z in range(N_Z):
        slots = slots_ref[:, z].reshape(N_DP * Q_ROWS, WIDE)
        rows = contract(select, slots, 1, 0).astype(jnp.bfloat16)
        for p in range(HEAD_PAIRS):
            out_ref[z, :, p * WIDE : (p + 1) * WIDE] = rows[p * SLAB : (p + 1) * SLAB]
        copy_out(z).start()
    for z in range(N_Z):
        copy_out(z).wait()


def call(kernel, name, outs, specs, flops, moved, exps=0, scratch=(), vmem=VMEM_BYTES, out_space=pltpu.VMEM):
    return pl.pallas_call(
        kernel,
        name=name,
        out_shape=[jax.ShapeDtypeStruct(shape, dtype) for shape, dtype in outs],
        in_specs=[pl.BlockSpec(memory_space=s) for s in specs],
        out_specs=[pl.BlockSpec(memory_space=out_space)] * len(outs),
        scratch_shapes=scratch,
        compiler_params=pltpu.CompilerParams(vmem_limit_bytes=vmem),
        cost_estimate=pl.CostEstimate(flops=flops, bytes_accessed=moved, transcendentals=exps),
    )


def exchange(blocks):
    flat = blocks.reshape((N_DP * N_Z,) + blocks.shape[2:])
    flat = lax.all_to_all(flat, EXCHANGE, split_axis=0, concat_axis=0, tiled=True)
    return flat.reshape(blocks.shape)


def local(query, key, value, doc_lengths, send_slots, slab_source, back_pack, back_index):
    V, S, H = pltpu.VMEM, pltpu.SMEM, pl.ANY
    half, whole = jnp.bfloat16, jnp.int32
    columns = GROUP_HEADS * SLAB
    q_blocks = (N_DP, N_Z, Q_ROWS, WIDE)
    kv_blocks = (N_DP, N_Z, KV_ROWS, WIDE)
    (kv_sent,) = call(
        pack_kv_kernel,
        "pack_kv",
        [(kv_blocks, half)],
        [H, H, H, H],
        2 * 10**8,
        2 * 10**6,
        0,
        [
            V((1, 1, SLAB), whole),
            V((1, 1, SLAB), whole),
            V((2 * SLAB, KEY_VALUE_HEADS * HEAD_SIZE), half),
            V((N_Z, N_DP, KV_ROWS, WIDE), half),
            pltpu.SemaphoreType.DMA((4,)),
            pltpu.SemaphoreType.DMA((N_Z,)),
        ],
        60 * 1024 * 1024,
        pl.ANY,
    )(back_index, slab_source, key, value)
    kv_slots = exchange(kv_sent)
    own_code = back_index.reshape(1, SLAB)
    (q_sent,) = call(pack_q_kernel, "pack_q", [(q_blocks, half)], [V, V], 8 * 10**8, 3 * 10**6)(
        own_code, query
    )
    sent = send_slots.reshape(N_DP, 1, CAP)
    run = jnp.arange(HEAD_PAIRS, dtype=whole).reshape(1, HEAD_PAIRS, 1)
    targets = jnp.where(sent < SLAB, sent + run * SLAB, -1).reshape(1, N_DP * Q_ROWS)
    q_sent, kv_slots, targets = lax.optimization_barrier((q_sent, kv_slots, targets))
    q_slots = exchange(q_sent)
    group = lax.axis_index(("y", "core")).astype(whole).reshape(1)
    kv_placed, code = call(
        place_kv_kernel,
        "place_kv",
        [((N_Z, 2 * SLAB, HEAD_SIZE), half), ((N_Z, SLAB), whole)],
        [S, V],
        2 * 10**8,
        2 * 10**6,
    )(group, kv_slots)
    lane = lax.axis_index("x").astype(whole).reshape(1)
    pieces = [kv_placed] + [
        lax.ppermute(kv_placed, "x", [(x, (x + back) % N_X) for x in range(N_X)])
        for back in range(1, N_X)
    ]
    f32 = jnp.float32
    (out_sent,) = call(
        attend_kernel,
        "attend",
        [(q_blocks, half)],
        [S, S, V] + [pl.ANY] * (1 + N_X),
        4 * 10**9,
        5 * 10**6,
        3 * 10**6,
        [
            V((N_Z, N_X, 2 * SLAB, HEAD_SIZE), half),
            V((N_Z, N_DP, Q_ROWS, WIDE), half),
            V((N_Z, N_DP, Q_ROWS, WIDE), half),
            V((N_Z, N_DP * Q_ROWS, HEAD_PAIRS * SLAB), half),
            V((N_Z, HEAD_SIZE, columns), half),
            V((MAX_ITEMS, PAIR, columns), f32),
            V((N_Z, 8, columns), f32),
            V((N_Z, 8, columns), f32),
            V((N_Z, HEAD_SIZE, columns), f32),
            S((N_Z,), whole),
            S((N_Z,), whole),
            pltpu.SemaphoreType.DMA((N_Z,)),
            pltpu.SemaphoreType.DMA((N_Z,)),
            pltpu.SemaphoreType.DMA((N_X,)),
        ],
        40 * 1024 * 1024,
        pl.ANY,
    )(doc_lengths.reshape(DOCS), lane, code, q_slots, *pieces)
    out_slots = exchange(out_sent)
    (out,) = call(
        unpack_kernel,
        "unpack",
        [((SLAB, QUERY_HEADS * HEAD_SIZE), half)],
        [V, V],
        8 * 10**8,
        3 * 10**6,
        0,
        [V((N_Z, SLAB, HEAD_PAIRS * WIDE), half), pltpu.SemaphoreType.DMA((N_Z,))],
        VMEM_BYTES,
        pl.ANY,
    )(targets, out_slots)
    return out


def solution(mesh):
    wide = Mesh(mesh.devices.reshape(N_DP // 2, 2, N_Z, N_X), ("y", "core", "z", "x"))
    rows = P(("y", "core", "z", "x"), None)
    table = P(("y", "core"), ("z", "x"), None)
    return jax.shard_map(
        local,
        mesh=wide,
        in_specs=(rows, rows, rows, P(("y", "core"), None, None), table, table, table, table),
        out_specs=rows,
        check_vma=False,
    )
```

```python
import math

import jax
import jax.numpy as jnp
from jax import lax
from jax.experimental import pallas as pl
from jax.experimental.pallas import tpu as pltpu
from jax.sharding import Mesh, PartitionSpec as P

QUERY_HEADS = 32
KEY_VALUE_HEADS = 8
HEAD_SIZE = 128
GROUP_HEADS = QUERY_HEADS // KEY_VALUE_HEADS
CAP = 12
N_DP = 16
N_Z = 8
N_X = 4
SLAB = 128
DOCS = 8
MOST = 2048
WIDE = 2 * HEAD_SIZE
HEAD_PAIRS = GROUP_HEADS // 2
Q_ROWS = HEAD_PAIRS * CAP
KV_ROWS = 16
PAIR = 2 * SLAB
SLAB_BITS = 7
MAX_ITEMS = 48
STEPS = (8, 2, 1)
EXP2_SCALE = math.log2(math.e) / math.sqrt(HEAD_SIZE)
MASKED = -1e30
VMEM_BYTES = 16 * 1024 * 1024
EXCHANGE = ("y", "core", "z")


def slot_rows(code, runs, block_rows):
    peer = (code * 171) >> 11
    base = peer * block_rows + (code - peer * CAP)
    return jnp.concatenate([base + run * CAP for run in range(runs)], axis=1)


def one_hot(rows, targets):
    at = lax.broadcasted_iota(jnp.int32, (rows, targets.shape[1]), 0)
    return jnp.where(at == targets, 1.0, 0.0).astype(jnp.bfloat16)


def contract(a, b, dim_a, dim_b):
    return lax.dot_general(
        a, b, (((dim_a,), (dim_b,)), ((), ())), preferred_element_type=jnp.float32
    )


def copy_slab(slabs_ref, blocks_hbm, sems, z):
    return pltpu.make_async_copy(slabs_ref.at[z], blocks_hbm.at[:, z], sems.at[z])


def pack_kv_kernel(
    code_ref, table_ref, key_ref, value_ref, out_hbm, code, table, rows, out_ref, sems, out_sems
):
    copies = [
        pltpu.make_async_copy(code_ref, code, sems.at[0]),
        pltpu.make_async_copy(table_ref, table, sems.at[1]),
        pltpu.make_async_copy(key_ref, rows.at[:SLAB], sems.at[2]),
        pltpu.make_async_copy(value_ref, rows.at[SLAB:], sems.at[3]),
    ]
    for copy in copies:
        copy.start()
    for copy in copies:
        copy.wait()
    select = one_hot(N_DP * KV_ROWS, slot_rows(code[0], 1, KV_ROWS))
    codes = table[0].astype(jnp.float32)
    at = lax.broadcasted_iota(jnp.int32, (N_DP * KV_ROWS, WIDE), 0) & (KV_ROWS - 1)
    codes = jnp.where(at >= CAP, jnp.concatenate([codes, codes], axis=1), 0.0)
    for z in range(N_Z):
        lanes = slice(z * HEAD_SIZE, (z + 1) * HEAD_SIZE)
        both = jnp.concatenate([rows[:SLAB, lanes], rows[SLAB:, lanes]], axis=1)
        sent = (contract(select, both, 1, 0) + codes).astype(jnp.bfloat16)
        out_ref[z] = sent.reshape(N_DP, KV_ROWS, WIDE)
        copy_slab(out_ref, out_hbm, out_sems, z).start()
    for z in range(N_Z):
        copy_slab(out_ref, out_hbm, out_sems, z).wait()


def pack_q_kernel(code_ref, query_ref, out_ref):
    select = one_hot(N_DP * Q_ROWS, slot_rows(code_ref[...], HEAD_PAIRS, Q_ROWS))
    for z in range(N_Z):
        first = z * HEAD_PAIRS
        rows = jnp.concatenate(
            [query_ref[:, (first + p) * WIDE : (first + p + 1) * WIDE] for p in range(HEAD_PAIRS)],
            axis=0,
        )
        sent = contract(select, rows, 1, 0).astype(jnp.bfloat16)
        out_ref[:, z] = sent.reshape(N_DP, Q_ROWS, WIDE)


def place_kv_kernel(group_ref, slots_ref, out_ref, code_ref):
    group = group_ref[0]
    for z in range(N_Z):
        own = slots_ref[group, z].astype(jnp.float32).astype(jnp.int32)
        code = own[CAP : CAP + 1, :SLAB]
        code_ref[z : z + 1, :] = code
        select = one_hot(N_DP * KV_ROWS, slot_rows(code, 1, KV_ROWS))
        slots = slots_ref[:, z].reshape(N_DP * KV_ROWS, WIDE)
        keys = contract(select, slots[:, :HEAD_SIZE], 0, 0)
        values_t = contract(slots[:, HEAD_SIZE:], select, 0, 0)
        out_ref[z, :SLAB] = keys.astype(jnp.bfloat16)
        out_ref[z, SLAB:] = values_t.astype(jnp.bfloat16)


def each_item(items, end_of, body):
    done, slab = jnp.int32(0), jnp.int32(0)
    for size in STEPS:
        steps = (items - done) // size if size > 1 else items - done

        def step(i, slab, done=done, size=size):
            for r in range(size):
                item = done + i * size + r
                slab = jnp.where(item >= end_of[slab], slab + 1, slab)
                body(item, slab)
            return slab

        slab = lax.fori_loop(0, steps, step, slab)
        done = done + steps * size


def attend_kernel(
    lengths_ref,
    lane_ref,
    code_ref,
    slots_ref,
    piece_0,
    piece_1,
    piece_2,
    piece_3,
    out_ref,
    kv_ref,
    select_ref,
    query_ref,
    scores_ref,
    tops_ref,
    sums_ref,
    acc_ref,
    low_of,
    end_of,
    piece_sems,
):
    lane = lane_ref[0]
    columns = GROUP_HEADS * SLAB

    pieces = [
        pltpu.make_async_copy(piece, kv_ref.at[:, (lane - back) & (N_X - 1)], piece_sems.at[back])
        for back, piece in enumerate((piece_0, piece_1, piece_2, piece_3))
    ]

    for piece in pieces:
        piece.start()

    bounds = []
    total = jnp.int32(0)
    for i in range(DOCS):
        total = total + lengths_ref[i]
        bounds.append(total)

    items = jnp.int32(0)
    for z in range(N_Z):
        first = (z * N_X + lane) * SLAB
        start = jnp.int32(0)
        for bound in bounds:
            start = jnp.where(first >= bound, bound, start)
        block = z * N_X + lane
        count = (block - (start >> SLAB_BITS) + 2) >> 1
        low_of[z] = block + 1 - 2 * count - 2 * items
        items = items + count
        end_of[z] = items

    @pl.loop(0, N_Z)
    def _(z):
        targets = slot_rows(code_ref[pl.ds(z, 1), :], HEAD_PAIRS, Q_ROWS)
        select_ref[z] = one_hot(N_DP * Q_ROWS, targets)
        tops_ref[z] = jnp.full((8, columns), MASKED, jnp.float32)
        sums_ref[z] = jnp.zeros((8, columns), jnp.float32)
        acc_ref[z] = jnp.zeros((HEAD_SIZE, columns), jnp.float32)
        slots = slots_ref[:, z].reshape(N_DP * Q_ROWS, WIDE)
        query_t = contract(slots, select_ref[z], 0, 0).astype(jnp.bfloat16)
        query_ref[z, :, : columns // 2] = query_t[:HEAD_SIZE]
        query_ref[z, :, columns // 2 :] = query_t[HEAD_SIZE:]

    for piece in pieces:
        piece.wait()

    def place(item, z):
        block = low_of[z] + 2 * item
        lower = jnp.maximum(block, 0)
        return block, (lower >> 2, lower & 3), ((block + 1) >> 2, (block + 1) & 3)

    in_slab = lax.broadcasted_iota(jnp.int32, (1, SLAB), 1)
    in_pair = lax.broadcasted_iota(jnp.int32, (PAIR, SLAB), 0)

    def score(item, z):
        block, one, two = place(item, z)
        query_at = (z * N_X + lane) * SLAB + in_slab
        start = jnp.zeros((1, SLAB), jnp.int32)
        for bound in bounds:
            start = jnp.where(query_at >= bound, bound, start)
        at = block * SLAB
        allowed = (in_pair >= start - at) & (in_pair <= query_at - at)
        keys = jnp.concatenate([kv_ref[*one, :SLAB], kv_ref[*two, :SLAB]], axis=0)
        s = contract(keys, query_ref[z], 1, 0) * EXP2_SCALE
        tops = []
        for h in range(GROUP_HEADS):
            lanes = slice(h * SLAB, (h + 1) * SLAB)
            masked = jnp.where(allowed, s[:, lanes], MASKED)
            scores_ref[item, :, lanes] = masked
            tops.append(jnp.max(masked.reshape(PAIR // 8, 8, SLAB), axis=0))
        tops_ref[z] = jnp.maximum(tops_ref[z], jnp.concatenate(tops, axis=1))

    each_item(items, end_of, score)

    @pl.loop(0, N_Z)
    def _(z):
        shift = jnp.max(tops_ref[z], axis=0, keepdims=True)
        tops_ref[z] = jnp.broadcast_to(shift, (8, columns))

    def weigh(item, z):
        _, one, two = place(item, z)
        weights = jnp.exp2(scores_ref[item] - tops_ref[z, :1])
        values_t = jnp.concatenate([kv_ref[*one, SLAB:], kv_ref[*two, SLAB:]], axis=1)
        acc_ref[z] += contract(values_t, weights.astype(jnp.bfloat16), 1, 0)
        sums_ref[z] += jnp.sum(weights.reshape(PAIR // 8, 8, columns), axis=0)

    each_item(items, end_of, weigh)

    @pl.loop(0, N_Z)
    def _(z):
        totals = jnp.sum(sums_ref[z], axis=0, keepdims=True)
        attended_t = (acc_ref[z] * (1.0 / totals)).astype(jnp.bfloat16)
        attended_t = jnp.concatenate(
            [attended_t[:, : columns // 2], attended_t[:, columns // 2 :]], axis=0
        )
        back = contract(select_ref[z], attended_t, 1, 1).astype(jnp.bfloat16)
        out_ref[:, z] = back.reshape(N_DP, Q_ROWS, WIDE)


def unpack_kernel(targets_ref, slots_ref, out_hbm, out_ref, sems):
    def copy_out(z):
        lanes = pl.ds(z * HEAD_PAIRS * WIDE, HEAD_PAIRS * WIDE)
        return pltpu.make_async_copy(out_ref.at[z], out_hbm.at[:, lanes], sems.at[z])

    select = one_hot(HEAD_PAIRS * SLAB, targets_ref[...])
    for z in range(N_Z):
        slots = slots_ref[:, z].reshape(N_DP * Q_ROWS, WIDE)
        rows = contract(select, slots, 1, 0).astype(jnp.bfloat16)
        for p in range(HEAD_PAIRS):
            out_ref[z, :, p * WIDE : (p + 1) * WIDE] = rows[p * SLAB : (p + 1) * SLAB]
        copy_out(z).start()
    for z in range(N_Z):
        copy_out(z).wait()


def call(kernel, name, outs, specs, flops, moved, exps=0, scratch=(), vmem=VMEM_BYTES, out_space=pltpu.VMEM):
    return pl.pallas_call(
        kernel,
        name=name,
        out_shape=[jax.ShapeDtypeStruct(shape, dtype) for shape, dtype in outs],
        in_specs=[pl.BlockSpec(memory_space=s) for s in specs],
        out_specs=[pl.BlockSpec(memory_space=out_space)] * len(outs),
        scratch_shapes=scratch,
        compiler_params=pltpu.CompilerParams(vmem_limit_bytes=vmem),
        cost_estimate=pl.CostEstimate(flops=flops, bytes_accessed=moved, transcendentals=exps),
    )


def exchange(blocks):
    flat = blocks.reshape((N_DP * N_Z,) + blocks.shape[2:])
    flat = lax.all_to_all(flat, EXCHANGE, split_axis=0, concat_axis=0, tiled=True)
    return flat.reshape(blocks.shape)


def local(query, key, value, doc_lengths, send_slots, slab_source, back_pack, back_index):
    V, S, H = pltpu.VMEM, pltpu.SMEM, pl.ANY
    half, whole = jnp.bfloat16, jnp.int32
    columns = GROUP_HEADS * SLAB
    q_blocks = (N_DP, N_Z, Q_ROWS, WIDE)
    kv_blocks = (N_DP, N_Z, KV_ROWS, WIDE)
    (kv_sent,) = call(
        pack_kv_kernel,
        "pack_kv",
        [(kv_blocks, half)],
        [H, H, H, H],
        2 * 10**8,
        2 * 10**6,
        0,
        [
            V((1, 1, SLAB), whole),
            V((1, 1, SLAB), whole),
            V((2 * SLAB, KEY_VALUE_HEADS * HEAD_SIZE), half),
            V((N_Z, N_DP, KV_ROWS, WIDE), half),
            pltpu.SemaphoreType.DMA((4,)),
            pltpu.SemaphoreType.DMA((N_Z,)),
        ],
        60 * 1024 * 1024,
        pl.ANY,
    )(back_index, slab_source, key, value)
    kv_slots = exchange(kv_sent)
    own_code = back_index.reshape(1, SLAB)
    (q_sent,) = call(pack_q_kernel, "pack_q", [(q_blocks, half)], [V, V], 8 * 10**8, 3 * 10**6)(
        own_code, query
    )
    sent = send_slots.reshape(N_DP, 1, CAP)
    run = jnp.arange(HEAD_PAIRS, dtype=whole).reshape(1, HEAD_PAIRS, 1)
    targets = jnp.where(sent < SLAB, sent + run * SLAB, -1).reshape(1, N_DP * Q_ROWS)
    q_sent, kv_slots, targets = lax.optimization_barrier((q_sent, kv_slots, targets))
    q_slots = exchange(q_sent)
    group = lax.axis_index(("y", "core")).astype(whole).reshape(1)
    kv_placed, code = call(
        place_kv_kernel,
        "place_kv",
        [((N_Z, 2 * SLAB, HEAD_SIZE), half), ((N_Z, SLAB), whole)],
        [S, V],
        2 * 10**8,
        2 * 10**6,
    )(group, kv_slots)
    lane = lax.axis_index("x").astype(whole).reshape(1)
    pieces = [kv_placed] + [
        lax.ppermute(kv_placed, "x", [(x, (x + back) % N_X) for x in range(N_X)])
        for back in range(1, N_X)
    ]
    f32 = jnp.float32
    (out_sent,) = call(
        attend_kernel,
        "attend",
        [(q_blocks, half)],
        [S, S, V, V] + [pl.ANY] * N_X,
        4 * 10**9,
        5 * 10**6,
        3 * 10**6,
        [
            V((N_Z, N_X, 2 * SLAB, HEAD_SIZE), half),
            V((N_Z, N_DP * Q_ROWS, HEAD_PAIRS * SLAB), half),
            V((N_Z, HEAD_SIZE, columns), half),
            V((MAX_ITEMS, PAIR, columns), f32),
            V((N_Z, 8, columns), f32),
            V((N_Z, 8, columns), f32),
            V((N_Z, HEAD_SIZE, columns), f32),
            S((N_Z,), whole),
            S((N_Z,), whole),
            pltpu.SemaphoreType.DMA((N_X,)),
        ],
        40 * 1024 * 1024,
    )(doc_lengths.reshape(DOCS), lane, code, q_slots, *pieces)
    out_slots = exchange(out_sent)
    (out,) = call(
        unpack_kernel,
        "unpack",
        [((SLAB, QUERY_HEADS * HEAD_SIZE), half)],
        [V, V],
        8 * 10**8,
        3 * 10**6,
        0,
        [V((N_Z, SLAB, HEAD_PAIRS * WIDE), half), pltpu.SemaphoreType.DMA((N_Z,))],
        VMEM_BYTES,
        pl.ANY,
    )(targets, out_slots)
    return out


def solution(mesh):
    wide = Mesh(mesh.devices.reshape(N_DP // 2, 2, N_Z, N_X), ("y", "core", "z", "x"))
    rows = P(("y", "core", "z", "x"), None)
    table = P(("y", "core"), ("z", "x"), None)
    return jax.shard_map(
        local,
        mesh=wide,
        in_specs=(rows, rows, rows, P(("y", "core"), None, None), table, table, table, table),
        out_specs=rows,
        check_vma=False,
    )
```
